256 devices in a mesh: chan: 64 (over z, y, core), panel: 4 (over x).
Axes of the slice: x: 4, y: 4, z: 8, core: 2. Of those that a mesh axis runs over, the one named last changes fastest.
Arguments:
- eta: bfloat16 [128, 1024, 1024], P('chan', 'panel'), as said below
- gamma: bfloat16 [128, 1024, 1024], P('chan', 'panel')
- pp_weight: float32 [128, 1024], P('chan'), may hold values from -1 to 1
- cc_weight: float32 [128, 1024], P('chan'), may hold values from -1 to 1
- live_pairs: int32 [128], P('chan'), may hold values from 256 to 1024, as said below
- forward_table: bfloat16 [128, 128], replicated, may hold values from -0.5 to 0.5
- back_table: bfloat16 [128, 128], replicated, may hold values from -0.5 to 0.5
Outputs:
- commutator: bfloat16 [128, 1024, 1024], P('chan', 'panel')
The draws below stay inside these ranges and needn't reach their ends.
Inputs may be any that keep to these rules, and one draw needn't show every extreme that they name: eta[j] is exactly antisymmetric and gamma[j] exactly symmetric for every channel j. `live_pairs`: each value is a multiple of 256.
All inputs are finite; a program needn't handle non-finite values.
Results may differ from the reference program's by a relative error of at most 0.0067.
Values may be sent and summed in bfloat16 or wider, within the bound.
No kernel may reach another device: no remote copies, remote signals or barrier semaphores. Data moves between devices by JAX's collectives and lax.ppermute only.
A program may use at most 128 MiB of HBM per device.

```python
import jax
import jax.numpy as jnp
from jax import lax

NORB = 32
PAIRS = 1024
CHANNELS = 128


def draw_eta(key, part):
    key = jax.random.fold_in(key, 11)
    shape = (CHANNELS, PAIRS, PAIRS)
    base = jax.random.normal(key, shape, jnp.float32)
    base = base * PAIRS ** (-0.25)
    return ((base - jnp.swapaxes(base, 1, 2)) * 0.7071).astype(jnp.bfloat16)


def draw_gamma(key, part):
    key = jax.random.fold_in(key, 23)
    shape = (CHANNELS, PAIRS, PAIRS)
    base = jax.random.normal(key, shape, jnp.float32)
    base = base * PAIRS ** (-0.25)
    return ((base + jnp.swapaxes(base, 1, 2)) * 0.7071).astype(jnp.bfloat16)


def draw_live_pairs(key, part):
    key = jax.random.fold_in(key, 37)
    steps = jax.random.randint(key, (CHANNELS,), 1, 5)
    steps = steps.at[0].set(4).at[1].set(1)
    return (steps * (PAIRS // 4)).astype(jnp.int32)


def steps_of(key, shape, split, smallest, high):
    level = 1.0
    for dim, shards_of in split:
        steps = jax.random.uniform(jax.random.fold_in(jax.random.fold_in(key, 6), dim), (shards_of,), jnp.float32, smallest / len(split), high / len(split))
        level = level * jnp.repeat(jnp.exp(steps), shape[dim] // shards_of).reshape((-1,) + (1,) * (len(shape) - 1 - dim))
    return level


def noise(own_key, extent, scale, bound, kind=jnp.bfloat16):
    drawn = scale * jax.random.normal(own_key, extent, jnp.float32)
    return jnp.clip(drawn, min=-bound, max=bound).astype(kind)


def setup_inputs(seed: int = 0) -> dict:
    key_of = jax.random.split(jax.random.key(seed), 8)
    eta = draw_eta(jax.random.fold_in(key_of[7], 71), 0)
    gamma = draw_gamma(jax.random.fold_in(key_of[7], 71), 0)
    pp_weight = jnp.clip(jax.random.uniform(key_of[2], (CHANNELS, PAIRS), jnp.float32, -1.0, 1.0) * steps_of(key_of[2], (CHANNELS, PAIRS), ((0, 64),), -0.4, 0.0), -1.0, 1.0)
    cc_weight = jnp.clip(jax.random.uniform(key_of[3], (CHANNELS, PAIRS), jnp.float32, -1.0, 1.0) * steps_of(key_of[3], (CHANNELS, PAIRS), ((0, 64),), -0.4, 0.0), -1.0, 1.0)
    live_pairs = draw_live_pairs(jax.random.fold_in(key_of[7], 71), 0)
    forward_table = noise(key_of[5], (CHANNELS, CHANNELS), CHANNELS ** -0.5, 0.5)
    back_table = noise(key_of[6], (CHANNELS, CHANNELS), CHANNELS ** -0.5, 0.5)
    return dict(eta=eta, gamma=gamma, pp_weight=pp_weight, cc_weight=cc_weight, live_pairs=live_pairs, forward_table=forward_table, back_table=back_table)


def swap_pairs(operand):
    count = operand.shape[0]
    shaped = operand.reshape(count, NORB, NORB, NORB, NORB)
    return shaped.transpose(0, 1, 4, 3, 2).reshape(operand.shape)


def recouple(operand, coupling):
    mixed = jnp.einsum("kj,jpq->kpq", coupling.astype(jnp.float32), operand.astype(jnp.float32))
    return mixed.astype(jnp.bfloat16)


def commute(anti_part, sym_part, weight):
    scaled = (anti_part.astype(jnp.float32) * weight[:, None, :]).astype(jnp.bfloat16)

    def product(pieces):
        return jnp.dot(pieces[0], pieces[1], preferred_element_type=jnp.float32)

    forward_term = lax.map(product, (scaled, sym_part))
    return forward_term + jnp.swapaxes(forward_term, 1, 2)


def reference(eta, gamma, pp_weight, cc_weight, live_pairs, forward_table, back_table):
    positions = lax.broadcasted_iota(jnp.int32, pp_weight.shape, 1)
    weight_pp = jnp.where(positions < live_pairs[:, None], pp_weight, jnp.float32(0.0))
    pp_part = commute(eta, gamma, weight_pp)
    eta_cc = swap_pairs(recouple(eta, forward_table))
    gamma_cc = swap_pairs(recouple(gamma, forward_table))
    cc_part = commute(eta_cc, gamma_cc, cc_weight).astype(jnp.bfloat16)
    back_part = recouple(swap_pairs(cc_part), back_table)
    return (pp_part + back_part.astype(jnp.float32)).astype(jnp.bfloat16)
```

```python
import jax
import jax.numpy as jnp
from jax import lax
from jax.experimental import pallas as pl
from jax.experimental.pallas import tpu as pltpu
from jax.sharding import PartitionSpec as P

BF16 = jnp.bfloat16
F32 = jnp.float32
OFFSETS = (0, 1, -2, 3, 4)
LANES = 128


def params():
    return pltpu.CompilerParams(vmem_limit_bytes=48 * 1024 * 1024)


def cost(flops, size):
    return pl.CostEstimate(flops=flops, bytes_accessed=size, transcendentals=0)


def tile_at(panel, l, offset):
    return pl.multiple_of(lax.rem(2 * panel + l + offset + 8, 8) * LANES, LANES)


def swap_blocks(x):
    lane = lax.broadcasted_iota(jnp.int32, (64, LANES), 1)
    top, bottom = x[:64], x[64:]
    low = lane < 64
    upper = jnp.where(low, top, pltpu.roll(bottom, 64, 1))
    lower = jnp.where(low, pltpu.roll(top, 64, 1), bottom)
    even = (lane[:32] & 32) == 0
    parts = []
    for half in (upper, lower):
        first, second = half[:32], half[32:]
        parts.append(jnp.where(even, first, pltpu.roll(second, 32, 1)))
        parts.append(jnp.where(even, pltpu.roll(first, 96, 1), second))
    return jnp.concatenate(parts, axis=0)


def contract_last(a, b):
    return lax.dot_general(a, b, (((1,), (1,)), ((), ())), preferred_element_type=F32)


def pack_kernel(eta_ref, gamma_ref, out_ref):
    panel = lax.axis_index("panel")
    for arr, ref in enumerate((eta_ref, gamma_ref)):
        for l in range(2):
            for t, offset in enumerate(OFFSETS):
                column = tile_at(panel, l, offset)
                rows = [ref[ch, l * 128 : (l + 1) * 128, pl.ds(column, LANES)].astype(F32).reshape(16, 8, LANES) for ch in range(2)]
                start = arr * 32 + l * 16
                out_ref[start : start + 16, t] = jnp.concatenate(rows, axis=1).astype(BF16)


def spread_kernel(forward_ref, back_ref, forward_out, back_out):
    for ref, out, shift in ((forward_ref, forward_out, 3), (back_ref, back_out, 2)):
        size = 128 << shift
        row = lax.broadcasted_iota(jnp.int32, (size, 128), 0) >> shift
        column = lax.broadcasted_iota(jnp.int32, (size, 128), 1)
        copies = jnp.where(row == column, F32(1.0), F32(0.0)).astype(BF16)
        tall = jnp.dot(copies, ref[...], preferred_element_type=F32).astype(BF16)
        mask = (1 << shift) - 1
        for start in range(0, size, 256):
            wide = contract_last(tall[start : start + 256], copies)
            row = lax.broadcasted_iota(jnp.int32, wide.shape, 0) & mask
            column = lax.broadcasted_iota(jnp.int32, wide.shape, 1) & mask
            out[start : start + 256, :] = jnp.where(row == column, wide, F32(0.0)).astype(BF16)


def recouple_kernel(table_ref, in_ref, out_ref):
    rhs = jnp.concatenate([in_ref[:, q].reshape(1024, LANES) for q in range(5)], axis=1)
    mixed = jnp.dot(table_ref[...], rhs, preferred_element_type=F32).astype(BF16)
    for q in range(5):
        out_ref[:, q] = mixed[:, q * LANES : (q + 1) * LANES].reshape(64, 16, LANES)


def tile_of(ref, arr, l, t, ch):
    start = arr * 32 + l * 16
    return ref[start : start + 16, t].astype(F32)[:, ch * 8 : ch * 8 + 8].reshape(128, LANES)


PLUS = ((1, 1), (0, 3))
MINUS = ((0, 2), (1, 2))
FAR = ((1, 3),)


def mirror_kernel(in_ref, plus_ref, minus_ref, far_ref):
    for arr in range(2):
        for ch in range(2):
            for ref, held in ((plus_ref, PLUS), (minus_ref, MINUS), (far_ref, FAR)):
                for u, (l, t) in enumerate(held):
                    ref[(arr * 2 + ch) * len(held) + u] = swap_blocks(tile_of(in_ref, arr, l, t, ch).T).astype(BF16)


def product_kernel(in_ref, plus_ref, minus_ref, far_ref, weight_ref, out_ref, scaled, plain):
    panel = lax.axis_index("panel")
    for ch in range(2):
        for l in range(2):
            weight = weight_ref[ch : ch + 1, pl.ds(tile_at(panel, l, 0), LANES)]

            def put(arr, offset, value):
                rows = pl.ds(tile_at(panel, l, offset), LANES)
                columns = slice(l * LANES, (l + 1) * LANES)
                if arr == 0:
                    scaled[ch, rows, columns] = (value * weight).astype(BF16)
                else:
                    plain[ch, rows, columns] = value.astype(BF16)

            for arr in range(2):
                base = arr * 2 + ch
                for t, offset in enumerate(OFFSETS):
                    tile = swap_blocks(tile_of(in_ref, arr, l, t, ch))
                    put(arr, offset, -tile if arr == 0 else tile)
                put(arr, 2, minus_ref[base * 2 + l].astype(F32))
                if l == 0:
                    put(arr, -1, plus_ref[base * 2].astype(F32))
                    put(arr, -3, far_ref[base].astype(F32))
                else:
                    put(arr, -1, swap_blocks(tile_of(in_ref, arr, 0, 1, ch).T))
                    put(arr, -3, plus_ref[base * 2 + 1].astype(F32))
        for owner in range(4):
            rows = slice(owner * 256, (owner + 1) * 256)
            total = contract_last(scaled[ch, rows], plain[ch]) + contract_last(plain[ch, rows], scaled[ch])
            for l in range(2):
                for t, offset in enumerate(OFFSETS):
                    column = (2 * owner + l + offset) % 8 * LANES
                    out_ref[owner, l, t, ch] = total[l * 128 : (l + 1) * 128, column : column + LANES].astype(BF16)


def sum_kernel(in_ref, out_ref):
    for l in range(2):
        low, high = [], []
        for t in range(5):
            both = []
            for ch in range(2):
                parts = [in_ref[p, l, t, ch].astype(F32) for p in range(4)]
                total = (parts[0] + parts[1]) + (parts[2] + parts[3])
                both.append(swap_blocks(total).reshape(16, 8, LANES))
            low += [both[0][:, :4], both[1][:, :4]]
            high += [both[0][:, 4:], both[1][:, 4:]]
        out_ref[l * 32 : l * 32 + 16] = jnp.concatenate(low, axis=1).astype(BF16)
        out_ref[l * 32 + 16 : l * 32 + 32] = jnp.concatenate(high, axis=1).astype(BF16)


def recouple_back_kernel(table_ref, in_ref, out_ref):
    value = in_ref[...].astype(F32)
    rhs = jnp.concatenate([value[:, q * 8 : q * 8 + 8].reshape(512, LANES) for q in range(5)], axis=1).astype(BF16)
    mixed = jnp.dot(table_ref[...], rhs, preferred_element_type=F32)
    pieces = [mixed[:, q * LANES : (q + 1) * LANES].reshape(64, 8, LANES) for q in range(5)]
    out_ref[...] = jnp.concatenate(pieces, axis=1).astype(BF16)


def back_tile(ref, l, t, ch):
    low = ref[l * 32 : l * 32 + 16].astype(F32)[:, t * 8 + ch * 4 : t * 8 + ch * 4 + 4]
    high = ref[l * 32 + 16 : l * 32 + 32].astype(F32)[:, t * 8 + ch * 4 : t * 8 + ch * 4 + 4]
    return jnp.concatenate([low, high], axis=1).reshape(128, LANES)


def back_mirror_kernel(in_ref, plus_ref, minus_ref, far_ref):
    for ch in range(2):
        for ref, held in ((plus_ref, PLUS), (minus_ref, MINUS), (far_ref, FAR)):
            for u, (l, t) in enumerate(held):
                ref[ch * len(held) + u] = back_tile(in_ref, l, t, ch).astype(BF16)


def finish_kernel(in_ref, plus_ref, minus_ref, far_ref, pp_ref, out_ref):
    panel = lax.axis_index("panel")
    for ch in range(2):
        for l in range(2):
            rows = slice(l * 128, (l + 1) * 128)

            def put(offset, value):
                columns = pl.ds(tile_at(panel, l, offset), LANES)
                out_ref[ch, rows, columns] = (pp_ref[ch, rows, columns] + value).astype(BF16)

            for t, offset in enumerate(OFFSETS):
                put(offset, back_tile(in_ref, l, t, ch).T)
            put(2, minus_ref[ch * 2 + l].astype(F32))
            if l == 0:
                put(-1, plus_ref[ch * 2].astype(F32))
                put(-3, far_ref[ch].astype(F32))
            else:
                put(-1, back_tile(in_ref, 0, 1, ch))
                put(-3, plus_ref[ch * 2 + 1].astype(F32))


def pair_kernel(eta_ref, gamma_ref, eta_all_ref, gamma_all_ref, weight_ref, out_ref):
    weight = weight_ref[0]
    own = (eta_ref[0].astype(F32) * weight).astype(BF16)
    other = (eta_all_ref[0].astype(F32) * weight).astype(BF16)
    out_ref[0] = contract_last(own, gamma_all_ref[0]) + contract_last(gamma_ref[0], other)


def pair_part(eta, gamma, eta_all, gamma_all, weight):
    step = 256
    return pl.pallas_call(
        pair_kernel,
        grid=(2, 1024 // step),
        in_specs=[
            pl.BlockSpec((1, 256, 1024), lambda c, q: (c, 0, 0)),
            pl.BlockSpec((1, 256, 1024), lambda c, q: (c, 0, 0)),
            pl.BlockSpec((1, step, 1024), lambda c, q: (c, q, 0)),
            pl.BlockSpec((1, step, 1024), lambda c, q: (c, q, 0)),
            pl.BlockSpec((1, 1, 1024), lambda c, q: (c, 0, 0)),
        ],
        out_specs=pl.BlockSpec((1, 256, step), lambda c, q: (c, 0, q)),
        out_shape=jax.ShapeDtypeStruct((2, 256, 1024), F32),
        compiler_params=params(),
        cost_estimate=cost(2 * 2 * 2 * 256 * 1024 * 1024, 12 * 1024 * 1024),
        name="pair_part",
    )(eta, gamma, eta_all, gamma_all, weight.reshape(2, 1, 1024))


def call(kernel, shapes, args, flops=0, scratch=(), name=None):
    single = not isinstance(shapes, list)
    outs = [shapes] if single else shapes
    shaped = [jax.ShapeDtypeStruct(s, BF16) for s in outs]
    size = sum(a.size * a.dtype.itemsize for a in args) + sum(2 * s.size for s in shaped)
    return pl.pallas_call(
        kernel,
        out_shape=shaped[0] if single else shaped,
        scratch_shapes=list(scratch),
        compiler_params=params(),
        cost_estimate=cost(flops, size),
        name=name,
    )(*args)


def exchange(operand, axis):
    return lax.all_to_all(operand, axis, split_axis=0, concat_axis=0, tiled=True)


def mirror(plus, minus, far):
    def step(value, by):
        return lax.ppermute(value, "panel", [(i, (i + by) % 4) for i in range(4)])

    return step(plus, 1), step(minus, 3), step(far, 2)


def shards(eta, gamma, pp_weight, cc_weight, live_pairs, forward_table, back_table):
    positions = lax.broadcasted_iota(jnp.int32, pp_weight.shape, 1)
    weight_pp = jnp.where(positions < live_pairs[:, None], pp_weight, F32(0.0))
    eta_all = lax.all_gather(eta, "panel", axis=1, tiled=True)
    gamma_all = lax.all_gather(gamma, "panel", axis=1, tiled=True)

    packed = call(pack_kernel, (64, 5, 16, LANES), (eta, gamma), name="pack")
    forward_wide, back_wide = call(spread_kernel, [(1024, 1024), (512, 512)], (forward_table, back_table), flops=600_000_000, name="spread")
    packed = exchange(packed, "chan")
    mixed = call(recouple_kernel, (64, 5, 16, LANES), (forward_wide, packed), flops=1_400_000_000, name="recouple")
    mixed = exchange(mixed, "chan")
    sends = call(mirror_kernel, [(8, 128, LANES), (8, 128, LANES), (4, 128, LANES)], (mixed,), name="mirror")
    received = mirror(*sends)
    partial = call(
        product_kernel,
        (4, 2, 5, 2, 128, LANES),
        (mixed, *received, cc_weight),
        flops=2_200_000_000,
        scratch=[pltpu.VMEM((2, 1024, 256), BF16)] * 2,
        name="product",
    )
    partial = exchange(partial, "panel")
    part = call(sum_kernel, (64, 40, LANES), (partial,), name="sum")
    part = exchange(part, "chan")
    part = call(recouple_back_kernel, (64, 40, LANES), (back_wide, part), flops=400_000_000, name="recouple_back")
    part = exchange(part, "chan")
    back_sends = call(back_mirror_kernel, [(4, 128, LANES), (4, 128, LANES), (2, 128, LANES)], (part,), name="back_mirror")
    back_received = mirror(*back_sends)
    pp_part = pair_part(eta, gamma, eta_all, gamma_all, weight_pp)
    return call(finish_kernel, (2, 256, 1024), (part, *back_received, pp_part), name="finish")


def solution(mesh):
    in_specs = (
        P("chan", "panel", None),
        P("chan", "panel", None),
        P("chan", None),
        P("chan", None),
        P("chan"),
        P(),
        P(),
    )
    out_specs = P("chan", "panel", None)
    return jax.shard_map(shards, mesh=mesh, in_specs=in_specs, out_specs=out_specs, check_vma=False)
```

```python
import jax
import jax.numpy as jnp
from jax import lax
from jax.experimental import pallas as pl
from jax.experimental.pallas import tpu as pltpu
from jax.sharding import PartitionSpec as P

BF16 = jnp.bfloat16
F32 = jnp.float32
OFFSETS = (0, 1, -2, 3, 4)
LANES = 128


def params():
    return pltpu.CompilerParams(vmem_limit_bytes=48 * 1024 * 1024)


def cost(flops, size):
    return pl.CostEstimate(flops=flops, bytes_accessed=size, transcendentals=0)


def tile_at(panel, l, offset):
    return pl.multiple_of(lax.rem(2 * panel + l + offset + 8, 8) * LANES, LANES)


def swap_blocks(x):
    lane = lax.broadcasted_iota(jnp.int32, (64, LANES), 1)
    top, bottom = x[:64], x[64:]
    low = lane < 64
    upper = jnp.where(low, top, pltpu.roll(bottom, 64, 1))
    lower = jnp.where(low, pltpu.roll(top, 64, 1), bottom)
    even = (lane[:32] & 32) == 0
    parts = []
    for half in (upper, lower):
        first, second = half[:32], half[32:]
        parts.append(jnp.where(even, first, pltpu.roll(second, 32, 1)))
        parts.append(jnp.where(even, pltpu.roll(first, 96, 1), second))
    return jnp.concatenate(parts, axis=0)


def contract_last(a, b):
    return lax.dot_general(a, b, (((1,), (1,)), ((), ())), preferred_element_type=F32)


def pack_kernel(eta_ref, gamma_ref, out_ref):
    panel = lax.axis_index("panel")
    for arr, ref in enumerate((eta_ref, gamma_ref)):
        for l in range(2):
            for t, offset in enumerate(OFFSETS):
                column = tile_at(panel, l, offset)
                rows = [ref[ch, l * 128 : (l + 1) * 128, pl.ds(column, LANES)].astype(F32).reshape(16, 8, LANES) for ch in range(2)]
                start = arr * 32 + l * 16
                out_ref[start : start + 16, t] = jnp.concatenate(rows, axis=1).astype(BF16)


def spread_kernel(forward_ref, back_ref, forward_out, back_out):
    for ref, out, shift in ((forward_ref, forward_out, 3), (back_ref, back_out, 2)):
        size = 128 << shift
        row = lax.broadcasted_iota(jnp.int32, (size, 128), 0) >> shift
        column = lax.broadcasted_iota(jnp.int32, (size, 128), 1)
        copies = jnp.where(row == column, F32(1.0), F32(0.0)).astype(BF16)
        tall = jnp.dot(copies, ref[...], preferred_element_type=F32).astype(BF16)
        mask = (1 << shift) - 1
        for start in range(0, size, 256):
            wide = contract_last(tall[start : start + 256], copies)
            row = lax.broadcasted_iota(jnp.int32, wide.shape, 0) & mask
            column = lax.broadcasted_iota(jnp.int32, wide.shape, 1) & mask
            out[start : start + 256, :] = jnp.where(row == column, wide, F32(0.0)).astype(BF16)


def recouple_kernel(table_ref, in_ref, out_ref):
    rhs = jnp.concatenate([in_ref[:, q].reshape(1024, LANES) for q in range(5)], axis=1)
    mixed = jnp.dot(table_ref[...], rhs, preferred_element_type=F32).astype(BF16)
    for q in range(5):
        out_ref[:, q] = mixed[:, q * LANES : (q + 1) * LANES].reshape(64, 16, LANES)


def tile_of(ref, arr, l, t, ch):
    start = arr * 32 + l * 16
    return ref[start : start + 16, t].astype(F32)[:, ch * 8 : ch * 8 + 8].reshape(128, LANES)


PLUS = ((1, 1), (0, 3))
MINUS = ((0, 2), (1, 2))
FAR = ((1, 3),)


def mirror_kernel(in_ref, plus_ref, minus_ref, far_ref):
    for arr in range(2):
        for ch in range(2):
            for ref, held in ((plus_ref, PLUS), (minus_ref, MINUS), (far_ref, FAR)):
                for u, (l, t) in enumerate(held):
                    ref[(arr * 2 + ch) * len(held) + u] = swap_blocks(tile_of(in_ref, arr, l, t, ch).T).astype(BF16)


def product_kernel(in_ref, plus_ref, minus_ref, far_ref, weight_ref, out_ref, scaled, plain):
    panel = lax.axis_index("panel")
    for ch in range(2):
        for l in range(2):
            weight = weight_ref[ch : ch + 1, pl.ds(tile_at(panel, l, 0), LANES)]

            def put(arr, offset, value):
                rows = pl.ds(tile_at(panel, l, offset), LANES)
                columns = slice(l * LANES, (l + 1) * LANES)
                if arr == 0:
                    scaled[ch, rows, columns] = (value * weight).astype(BF16)
                else:
                    plain[ch, rows, columns] = value.astype(BF16)

            for arr in range(2):
                base = arr * 2 + ch
                for t, offset in enumerate(OFFSETS):
                    tile = swap_blocks(tile_of(in_ref, arr, l, t, ch))
                    put(arr, offset, -tile if arr == 0 else tile)
                put(arr, 2, minus_ref[base * 2 + l].astype(F32))
                if l == 0:
                    put(arr, -1, plus_ref[base * 2].astype(F32))
                    put(arr, -3, far_ref[base].astype(F32))
                else:
                    put(arr, -1, swap_blocks(tile_of(in_ref, arr, 0, 1, ch).T))
                    put(arr, -3, plus_ref[base * 2 + 1].astype(F32))
        for owner in range(4):
            rows = slice(owner * 256, (owner + 1) * 256)
            total = contract_last(scaled[ch, rows], plain[ch]) + contract_last(plain[ch, rows], scaled[ch])
            for l in range(2):
                for t, offset in enumerate(OFFSETS):
                    column = (2 * owner + l + offset) % 8 * LANES
                    out_ref[owner, l, t, ch] = total[l * 128 : (l + 1) * 128, column : column + LANES].astype(BF16)


def sum_kernel(in_ref, out_ref):
    for l in range(2):
        low, high = [], []
        for t in range(5):
            both = []
            for ch in range(2):
                parts = [in_ref[p, l, t, ch].astype(F32) for p in range(4)]
                total = (parts[0] + parts[1]) + (parts[2] + parts[3])
                both.append(swap_blocks(total).reshape(16, 8, LANES))
            low += [both[0][:, :4], both[1][:, :4]]
            high += [both[0][:, 4:], both[1][:, 4:]]
        out_ref[l * 32 : l * 32 + 16] = jnp.concatenate(low, axis=1).astype(BF16)
        out_ref[l * 32 + 16 : l * 32 + 32] = jnp.concatenate(high, axis=1).astype(BF16)


def recouple_back_kernel(table_ref, in_ref, out_ref):
    value = in_ref[...].astype(F32)
    rhs = jnp.concatenate([value[:, q * 8 : q * 8 + 8].reshape(512, LANES) for q in range(5)], axis=1).astype(BF16)
    mixed = jnp.dot(table_ref[...], rhs, preferred_element_type=F32)
    pieces = [mixed[:, q * LANES : (q + 1) * LANES].reshape(64, 8, LANES) for q in range(5)]
    out_ref[...] = jnp.concatenate(pieces, axis=1).astype(BF16)


def back_tile(ref, l, t, ch):
    low = ref[l * 32 : l * 32 + 16].astype(F32)[:, t * 8 + ch * 4 : t * 8 + ch * 4 + 4]
    high = ref[l * 32 + 16 : l * 32 + 32].astype(F32)[:, t * 8 + ch * 4 : t * 8 + ch * 4 + 4]
    return jnp.concatenate([low, high], axis=1).reshape(128, LANES)


def back_mirror_kernel(in_ref, pp_ref, plus_ref, minus_ref, far_ref):
    for ch in range(2):
        for ref, held in ((plus_ref, PLUS), (minus_ref, MINUS), (far_ref, FAR)):
            for u, (l, t) in enumerate(held):
                ref[ch * len(held) + u] = (pp_ref[l, t, ch].T + back_tile(in_ref, l, t, ch)).astype(BF16)


def finish_kernel(in_ref, plus_ref, minus_ref, far_ref, pp_ref, out_ref):
    panel = lax.axis_index("panel")
    for ch in range(2):
        for l in range(2):

            def put(offset, value):
                out_ref[ch, l * 128 : (l + 1) * 128, pl.ds(tile_at(panel, l, offset), LANES)] = value.astype(BF16)

            for t, offset in enumerate(OFFSETS):
                put(offset, pp_ref[l, t, ch] + back_tile(in_ref, l, t, ch).T)
            put(2, minus_ref[ch * 2 + l])
            if l == 0:
                put(-1, plus_ref[ch * 2])
                put(-3, far_ref[ch])
            else:
                put(-1, pp_ref[0, 1, ch].T + back_tile(in_ref, 0, 1, ch))
                put(-3, plus_ref[ch * 2 + 1])


def contract_first(a, b):
    return lax.dot_general(a, b, (((0,), (0,)), ((), ())), preferred_element_type=F32)


def pair_kernel(eta_ref, gamma_ref, weight_ref, own_ref, plus_ref, far_ref, minus_ref, scaled, plain):
    panel = lax.axis_index("panel")
    for ch in range(2):
        for l in range(2):
            row = weight_ref[ch : ch + 1, pl.ds(tile_at(panel, l, 0), LANES)]
            weight = jnp.broadcast_to(row, (128, LANES)).T
            rows = slice(l * 128, (l + 1) * 128)
            for j in range(8):
                source = pl.ds(tile_at(panel, j, 0), LANES)
                columns = slice(j * LANES, (j + 1) * LANES)
                scaled[ch, rows, columns] = (eta_ref[ch, rows, source].astype(F32) * weight).astype(BF16)
                plain[ch, rows, columns] = gamma_ref[ch, rows, source]
        for owner, ref in enumerate((own_ref, plus_ref, far_ref, minus_ref)):
            columns = slice(owner * 256, (owner + 1) * 256)
            total = contract_first(scaled[ch, :, columns], plain[ch]) + contract_first(plain[ch, :, columns], scaled[ch])
            for l in range(2):
                for t, offset in enumerate(OFFSETS):
                    column = (2 * owner + l + offset) % 8 * LANES
                    ref[l, t, ch] = -total[l * 128 : (l + 1) * 128, column : column + LANES].astype(BF16)


def pair_sum_kernel(own_ref, plus_ref, far_ref, minus_ref, out_ref):
    for l in range(2):
        for t in range(5):
            for ch in range(2):
                parts = [ref[l, t, ch].astype(F32) for ref in (own_ref, plus_ref, far_ref, minus_ref)]
                out_ref[l, t, ch] = (parts[0] + parts[1]) + (parts[2] + parts[3])


def call(kernel, shapes, args, flops=0, scratch=(), name=None, dtype=BF16):
    single = not isinstance(shapes, list)
    outs = [shapes] if single else shapes
    shaped = [jax.ShapeDtypeStruct(s, dtype) for s in outs]
    size = sum(a.size * a.dtype.itemsize for a in args) + sum(2 * s.size for s in shaped)
    return pl.pallas_call(
        kernel,
        out_shape=shaped[0] if single else shaped,
        scratch_shapes=list(scratch),
        compiler_params=params(),
        cost_estimate=cost(flops, size),
        name=name,
    )(*args)


def exchange(operand, axis):
    return lax.all_to_all(operand, axis, split_axis=0, concat_axis=0, tiled=True)


def mirror(plus, minus, far):
    def step(value, by):
        return lax.ppermute(value, "panel", [(i, (i + by) % 4) for i in range(4)])

    return step(plus, 1), step(minus, 3), step(far, 2)


def shards(eta, gamma, pp_weight, cc_weight, live_pairs, forward_table, back_table):
    positions = lax.broadcasted_iota(jnp.int32, pp_weight.shape, 1)
    weight_pp = jnp.where(positions < live_pairs[:, None], pp_weight, F32(0.0))
    packed = call(pack_kernel, (64, 5, 16, LANES), (eta, gamma), name="pack")
    forward_wide, back_wide = call(spread_kernel, [(1024, 1024), (512, 512)], (forward_table, back_table), flops=600_000_000, name="spread")
    packed = exchange(packed, "chan")
    pp = call(
        pair_kernel,
        [(2, 5, 2, 128, LANES)] * 4,
        (eta, gamma, weight_pp),
        flops=2_200_000_000,
        scratch=[pltpu.VMEM((2, 256, 1024), BF16)] * 2,
        name="pair",
    )
    packed, *pp = lax.optimization_barrier((packed, *pp))
    mixed = call(recouple_kernel, (64, 5, 16, LANES), (forward_wide, packed), flops=1_400_000_000, name="recouple")
    mixed = exchange(mixed, "chan")
    pp_received = mirror(pp[1], pp[3], pp[2])
    pp_part = call(pair_sum_kernel, (2, 5, 2, 128, LANES), (pp[0], *pp_received), name="pair_sum", dtype=F32)
    mixed, pp_part = lax.optimization_barrier((mixed, pp_part))
    sends = call(mirror_kernel, [(8, 128, LANES), (8, 128, LANES), (4, 128, LANES)], (mixed,), name="mirror")
    received = mirror(*sends)
    partial = call(
        product_kernel,
        (4, 2, 5, 2, 128, LANES),
        (mixed, *received, cc_weight),
        flops=2_200_000_000,
        scratch=[pltpu.VMEM((2, 1024, 256), BF16)] * 2,
        name="product",
    )
    partial = exchange(partial, "panel")
    part = call(sum_kernel, (64, 40, LANES), (partial,), name="sum")
    part = exchange(part, "chan")
    part = call(recouple_back_kernel, (64, 40, LANES), (back_wide, part), flops=400_000_000, name="recouple_back")
    part = exchange(part, "chan")
    back_sends = call(back_mirror_kernel, [(4, 128, LANES), (4, 128, LANES), (2, 128, LANES)], (part, pp_part), name="back_mirror")
    back_received = mirror(*back_sends)
    return call(finish_kernel, (2, 256, 1024), (part, *back_received, pp_part), name="finish")


def solution(mesh):
    in_specs = (
        P("chan", "panel", None),
        P("chan", "panel", None),
        P("chan", None),
        P("chan", None),
        P("chan"),
        P(),
        P(),
    )
    out_specs = P("chan", "panel", None)
    return jax.shard_map(shards, mesh=mesh, in_specs=in_specs, out_specs=out_specs, check_vma=False)
```

```python
import jax
import jax.numpy as jnp
from jax import lax
from jax.experimental import pallas as pl
from jax.experimental.pallas import tpu as pltpu
from jax.sharding import PartitionSpec as P

BF16 = jnp.bfloat16
F32 = jnp.float32
OFFSETS = (0, 1, -2, 3, 4)
LANES = 128


def params():
    return pltpu.CompilerParams(vmem_limit_bytes=48 * 1024 * 1024)


def cost(flops, size):
    return pl.CostEstimate(flops=flops, bytes_accessed=size, transcendentals=0)


def tile_at(panel, l, offset):
    return pl.multiple_of(lax.rem(2 * panel + l + offset + 8, 8) * LANES, LANES)


def swap_blocks(x):
    lane = lax.broadcasted_iota(jnp.int32, (64, LANES), 1)
    top, bottom = x[:64], x[64:]
    low = lane < 64
    upper = jnp.where(low, top, pltpu.roll(bottom, 64, 1))
    lower = jnp.where(low, pltpu.roll(top, 64, 1), bottom)
    even = (lane[:32] & 32) == 0
    parts = []
    for half in (upper, lower):
        first, second = half[:32], half[32:]
        parts.append(jnp.where(even, first, pltpu.roll(second, 32, 1)))
        parts.append(jnp.where(even, pltpu.roll(first, 96, 1), second))
    return jnp.concatenate(parts, axis=0)


def contract_last(a, b):
    return lax.dot_general(a, b, (((1,), (1,)), ((), ())), preferred_element_type=F32)


def pack_kernel(eta_ref, gamma_ref, out_ref):
    panel = lax.axis_index("panel")
    for arr, ref in enumerate((eta_ref, gamma_ref)):
        for l in range(2):
            for t, offset in enumerate(OFFSETS):
                column = tile_at(panel, l, offset)
                rows = [ref[ch, l * 128 : (l + 1) * 128, pl.ds(column, LANES)].astype(F32).reshape(16, 8, LANES) for ch in range(2)]
                start = arr * 32 + l * 16
                out_ref[start : start + 16, t] = jnp.concatenate(rows, axis=1).astype(BF16)


def spread_kernel(forward_ref, back_ref, forward_out, back_out):
    for ref, out, shift in ((forward_ref, forward_out, 3), (back_ref, back_out, 2)):
        size = 128 << shift
        row = lax.broadcasted_iota(jnp.int32, (size, 128), 0) >> shift
        column = lax.broadcasted_iota(jnp.int32, (size, 128), 1)
        copies = jnp.where(row == column, F32(1.0), F32(0.0)).astype(BF16)
        tall = jnp.dot(copies, ref[...], preferred_element_type=F32).astype(BF16)
        mask = (1 << shift) - 1
        for start in range(0, size, 256):
            wide = contract_last(tall[start : start + 256], copies)
            row = lax.broadcasted_iota(jnp.int32, wide.shape, 0) & mask
            column = lax.broadcasted_iota(jnp.int32, wide.shape, 1) & mask
            out[start : start + 256, :] = jnp.where(row == column, wide, F32(0.0)).astype(BF16)


def recouple_kernel(table_ref, in_ref, out_ref):
    rhs = jnp.concatenate([in_ref[:, q].reshape(1024, LANES) for q in range(5)], axis=1)
    mixed = jnp.dot(table_ref[...], rhs, preferred_element_type=F32).astype(BF16)
    for q in range(5):
        out_ref[:, q] = mixed[:, q * LANES : (q + 1) * LANES].reshape(64, 16, LANES)


def tile_of(ref, arr, l, t, ch):
    start = arr * 32 + l * 16
    return ref[start : start + 16, t].astype(F32)[:, ch * 8 : ch * 8 + 8].reshape(128, LANES)


PLUS = ((1, 1), (0, 3))
MINUS = ((0, 2), (1, 2))
FAR = ((1, 3),)


def mirror_kernel(in_ref, plus_ref, minus_ref, far_ref):
    for arr in range(2):
        for ch in range(2):
            base = arr * 2 + ch
            for u, (l, t) in enumerate(PLUS + ((0, 4), (1, 3))):
                plus_ref[base * 4 + u] = swap_blocks(tile_of(in_ref, arr, l, t, ch).T).astype(BF16)
            for u, (l, t) in enumerate(MINUS):
                minus_ref[base * 4 + u] = swap_blocks(tile_of(in_ref, arr, l, t, ch).T).astype(BF16)
            for u, (l, t) in enumerate(((1, 3), (1, 4))):
                tile = swap_blocks(tile_of(in_ref, arr, l, t, ch))
                minus_ref[base * 4 + 2 + u] = (-tile if arr == 0 else tile).astype(BF16)
            for u, (l, t) in enumerate(FAR):
                far_ref[base + u] = swap_blocks(tile_of(in_ref, arr, l, t, ch).T).astype(BF16)


def product_kernel(
    in_ref, plus_ref, minus_ref, far_ref, weight_ref, own_ref, plus_out, far_out, minus_out, by_lane, by_row, plain, edge_lane, edge_row, edge_plain
):
    panel = lax.axis_index("panel")
    for ch in range(2):
        lanes = [weight_ref[ch : ch + 1, pl.ds(tile_at(panel, j, 0), LANES)] for j in range(8)]
        rows = [jnp.broadcast_to(lane, (128, LANES)).T for lane in lanes]
        for l in range(2):

            def put(arr, offset, value):
                j = (l + offset) % 8
                place = (slice(j * 128, (j + 1) * 128), slice(l * LANES, (l + 1) * LANES))
                if arr == 0:
                    by_lane.at[ch][place] = (value * lanes[l]).astype(BF16)
                    by_row.at[ch][place] = (value * rows[j]).astype(BF16)
                else:
                    plain.at[ch][place] = value.astype(BF16)

            for arr in range(2):
                base = arr * 2 + ch
                for t, offset in enumerate(OFFSETS):
                    tile = swap_blocks(tile_of(in_ref, arr, l, t, ch))
                    put(arr, offset, -tile if arr == 0 else tile)
                put(arr, 2, minus_ref[base * 4 + l].astype(F32))
                if l == 0:
                    put(arr, -1, plus_ref[base * 4].astype(F32))
                    put(arr, -3, far_ref[base].astype(F32))
                else:
                    put(arr, -1, swap_blocks(tile_of(in_ref, arr, 0, 1, ch).T))
                    put(arr, -3, plus_ref[base * 4 + 1].astype(F32))
        for arr in range(2):
            base = arr * 4 * 2 + ch * 4
            for r in range(2):
                for c in range(2):
                    ref = plus_ref if c == 0 else minus_ref
                    value = ref[base + 2 + r].astype(F32)
                    place = (slice(r * 128, (r + 1) * 128), slice(c * LANES, (c + 1) * LANES))
                    if arr == 0:
                        edge_lane.at[ch][place] = (value * lanes[2 + c]).astype(BF16)
                        edge_row.at[ch][place] = (value * rows[6 + r]).astype(BF16)
                    else:
                        edge_plain.at[ch][place] = value.astype(BF16)

        def block(ref, j):
            return ref[ch, j * 256 : (j + 1) * 256]

        def inner(i, j):
            return contract_last(block(by_lane, i), block(plain, j)) + contract_last(block(plain, i), block(by_lane, j))

        def tile(value, i, j):
            return value[i * 128 : (i + 1) * 128, j * 128 : (j + 1) * 128]

        diagonal = contract_first(by_row[ch], plain[ch]) + contract_first(plain[ch], by_row[ch])
        for (l, t), (i, j) in (((0, 0), (0, 0)), ((0, 1), (0, 1)), ((1, 0), (1, 1))):
            own_ref[l, t, ch] = -tile(diagonal, i, j)
        ahead = inner(0, 1) - contract_first(block(by_row, 3), edge_plain[ch]) - contract_first(block(plain, 3), edge_row[ch])
        own_ref[0, 3, ch] = tile(ahead, 0, 1)
        own_ref[1, 1, ch] = tile(ahead, 1, 0)
        plus_out[ch, 0] = tile(ahead, 0, 0).astype(BF16)
        plus_out[ch, 1] = tile(ahead, 1, 1).astype(BF16)
        behind = inner(3, 0) + jnp.dot(edge_lane[ch], block(plain, 1), preferred_element_type=F32) - jnp.dot(edge_plain[ch], block(by_row, 1), preferred_element_type=F32)
        own_ref[0, 2, ch] = tile(behind, 0, 0)
        own_ref[1, 2, ch] = tile(behind, 1, 1)
        minus_out[ch, 0] = tile(behind, 0, 1).astype(BF16)
        minus_out[ch, 1] = tile(behind, 1, 0).astype(BF16)
        across = inner(0, 2)
        for (l, t), (i, j) in ACROSS:
            own_ref[l, t, ch] = tile(across, i, j)
        for ref, start, value in ((far_out, 0, inner(2, 0)), (minus_out, 2, inner(3, 1)), (plus_out, 2, inner(1, 3))):
            for u, (held, (i, j)) in enumerate(ACROSS):
                ref[ch, start + u] = tile(value, i, j).astype(BF16)


ACROSS = (((0, 4), (0, 0)), ((1, 3), (1, 0)), ((1, 4), (1, 1)))


def sum_kernel(own_ref, plus_ref, far_ref, minus_ref, out_ref):
    def total(l, t, ch):
        value = own_ref[l, t, ch]
        if t == 2:
            return (value + plus_ref[ch, l].astype(F32)).T
        if (l, t) in ((0, 3), (1, 1)):
            return value + minus_ref[ch, l].astype(F32)
        for u, (held, _) in enumerate(ACROSS):
            if held == (l, t):
                near = plus_ref[ch, 2 + u].astype(F32) + minus_ref[ch, 2 + u].astype(F32)
                return value + far_ref[ch, u].astype(F32) + near
        return value

    for l in range(2):
        low, high = [], []
        for t in range(5):
            both = [swap_blocks(total(l, t, ch)).reshape(16, 8, LANES) for ch in range(2)]
            low += [both[0][:, :4], both[1][:, :4]]
            high += [both[0][:, 4:], both[1][:, 4:]]
        out_ref[l * 32 : l * 32 + 16] = jnp.concatenate(low, axis=1).astype(BF16)
        out_ref[l * 32 + 16 : l * 32 + 32] = jnp.concatenate(high, axis=1).astype(BF16)


def recouple_back_kernel(table_ref, in_ref, out_ref):
    value = in_ref[...].astype(F32)
    rhs = jnp.concatenate([value[:, q * 8 : q * 8 + 8].reshape(512, LANES) for q in range(5)], axis=1).astype(BF16)
    mixed = jnp.dot(table_ref[...], rhs, preferred_element_type=F32)
    pieces = [mixed[:, q * LANES : (q + 1) * LANES].reshape(64, 8, LANES) for q in range(5)]
    out_ref[...] = jnp.concatenate(pieces, axis=1).astype(BF16)


def back_tile(ref, l, t, ch):
    low = ref[l * 32 : l * 32 + 16].astype(F32)[:, t * 8 + ch * 4 : t * 8 + ch * 4 + 4]
    high = ref[l * 32 + 16 : l * 32 + 32].astype(F32)[:, t * 8 + ch * 4 : t * 8 + ch * 4 + 4]
    return jnp.concatenate([low, high], axis=1).reshape(128, LANES)


def back_mirror_kernel(in_ref, pp_ref, plus_ref, minus_ref, far_ref):
    for ch in range(2):
        for ref, held in ((plus_ref, PLUS), (minus_ref, MINUS), (far_ref, FAR)):
            for u, (l, t) in enumerate(held):
                ref[ch * len(held) + u] = (pp_ref[l, t, ch].T + back_tile(in_ref, l, t, ch)).astype(BF16)


def finish_kernel(in_ref, plus_ref, minus_ref, far_ref, pp_ref, out_ref):
    panel = lax.axis_index("panel")
    for ch in range(2):
        for l in range(2):

            def put(offset, value):
                out_ref[ch, l * 128 : (l + 1) * 128, pl.ds(tile_at(panel, l, offset), LANES)] = value.astype(BF16)

            for t, offset in enumerate(OFFSETS):
                put(offset, pp_ref[l, t, ch] + back_tile(in_ref, l, t, ch).T)
            put(2, minus_ref[ch * 2 + l])
            if l == 0:
                put(-1, plus_ref[ch * 2])
                put(-3, far_ref[ch])
            else:
                put(-1, pp_ref[0, 1, ch].T + back_tile(in_ref, 0, 1, ch))
                put(-3, plus_ref[ch * 2 + 1])


def contract_first(a, b):
    return lax.dot_general(a, b, (((0,), (0,)), ((), ())), preferred_element_type=F32)


def pair_kernel(eta_ref, gamma_ref, weight_ref, own_ref, plus_ref, far_ref, minus_ref, scaled, plain):
    panel = lax.axis_index("panel")
    for ch in range(2):
        for l in range(2):
            row = weight_ref[ch : ch + 1, pl.ds(tile_at(panel, l, 0), LANES)]
            weight = jnp.broadcast_to(row, (128, LANES)).T
            rows = slice(l * 128, (l + 1) * 128)
            for j in range(8):
                source = pl.ds(tile_at(panel, j, 0), LANES)
                columns = slice(j * LANES, (j + 1) * LANES)
                scaled[ch, rows, columns] = (eta_ref[ch, rows, source].astype(F32) * weight).astype(BF16)
                plain[ch, rows, columns] = gamma_ref[ch, rows, source]
        for owner, ref in enumerate((own_ref, plus_ref, far_ref, minus_ref)):
            columns = slice(owner * 256, (owner + 1) * 256)
            total = contract_first(scaled[ch, :, columns], plain[ch]) + contract_first(plain[ch, :, columns], scaled[ch])
            for l in range(2):
                for t, offset in enumerate(OFFSETS):
                    column = (2 * owner + l + offset) % 8 * LANES
                    ref[l, t, ch] = -total[l * 128 : (l + 1) * 128, column : column + LANES].astype(BF16)


def pair_sum_kernel(own_ref, plus_ref, far_ref, minus_ref, out_ref):
    for l in range(2):
        for t in range(5):
            for ch in range(2):
                parts = [ref[l, t, ch].astype(F32) for ref in (own_ref, plus_ref, far_ref, minus_ref)]
                out_ref[l, t, ch] = (parts[0] + parts[1]) + (parts[2] + parts[3])


def call(kernel, shapes, args, flops=0, scratch=(), name=None, dtype=BF16):
    single = not isinstance(shapes, list)
    outs = [shapes] if single else shapes
    types = dtype if isinstance(dtype, list) else [dtype] * len(outs)
    shaped = [jax.ShapeDtypeStruct(s, d) for s, d in zip(outs, types)]
    size = sum(a.size * a.dtype.itemsize for a in [*args, *shaped])
    return pl.pallas_call(
        kernel,
        out_shape=shaped[0] if single else shaped,
        scratch_shapes=list(scratch),
        compiler_params=params(),
        cost_estimate=cost(flops, size),
        name=name,
    )(*args)


def exchange(operand, axis):
    return lax.all_to_all(operand, axis, split_axis=0, concat_axis=0, tiled=True)


def mirror(plus, minus, far):
    def step(value, by):
        return lax.ppermute(value, "panel", [(i, (i + by) % 4) for i in range(4)])

    return step(plus, 1), step(minus, 3), step(far, 2)


def shards(eta, gamma, pp_weight, cc_weight, live_pairs, forward_table, back_table):
    positions = lax.broadcasted_iota(jnp.int32, pp_weight.shape, 1)
    weight_pp = jnp.where(positions < live_pairs[:, None], pp_weight, F32(0.0))
    packed = call(pack_kernel, (64, 5, 16, LANES), (eta, gamma), name="pack")
    forward_wide, back_wide = call(spread_kernel, [(1024, 1024), (512, 512)], (forward_table, back_table), flops=600_000_000, name="spread")
    packed = exchange(packed, "chan")
    pp = call(
        pair_kernel,
        [(2, 5, 2, 128, LANES)] * 4,
        (eta, gamma, weight_pp),
        flops=2_200_000_000,
        scratch=[pltpu.VMEM((2, 256, 1024), BF16)] * 2,
        name="pair",
    )
    packed, *pp = lax.optimization_barrier((packed, *pp))
    mixed = call(recouple_kernel, (64, 5, 16, LANES), (forward_wide, packed), flops=1_400_000_000, name="recouple")
    mixed = exchange(mixed, "chan")
    pp_received = mirror(pp[1], pp[3], pp[2])
    pp_part = call(pair_sum_kernel, (2, 5, 2, 128, LANES), (pp[0], *pp_received), name="pair_sum", dtype=F32)
    mixed, pp_part = lax.optimization_barrier((mixed, pp_part))
    sends = call(mirror_kernel, [(16, 128, LANES), (16, 128, LANES), (4, 128, LANES)], (mixed,), name="mirror")
    received = mirror(*sends)
    own, *partial = call(
        product_kernel,
        [(2, 5, 2, 128, LANES), (2, 5, 128, LANES), (2, 3, 128, LANES), (2, 5, 128, LANES)],
        (mixed, *received, cc_weight),
        flops=1_400_000_000,
        scratch=[pltpu.VMEM((2, 1024, 256), BF16)] * 3 + [pltpu.VMEM((2, 256, 256), BF16)] * 3,
        name="product",
        dtype=[F32, BF16, BF16, BF16],
    )
    plus, minus, far = mirror(partial[0], partial[2], partial[1])
    part = call(sum_kernel, (64, 40, LANES), (own, plus, far, minus), name="sum")
    part = exchange(part, "chan")
    part = call(recouple_back_kernel, (64, 40, LANES), (back_wide, part), flops=400_000_000, name="recouple_back")
    part = exchange(part, "chan")
    back_sends = call(back_mirror_kernel, [(4, 128, LANES), (4, 128, LANES), (2, 128, LANES)], (part, pp_part), name="back_mirror")
    back_received = mirror(*back_sends)
    return call(finish_kernel, (2, 256, 1024), (part, *back_received, pp_part), name="finish")


def solution(mesh):
    in_specs = (
        P("chan", "panel", None),
        P("chan", "panel", None),
        P("chan", None),
        P("chan", None),
        P("chan"),
        P(),
        P(),
    )
    out_specs = P("chan", "panel", None)
    return jax.shard_map(shards, mesh=mesh, in_specs=in_specs, out_specs=out_specs, check_vma=False)
```

```python
import jax
import jax.numpy as jnp
from jax import lax
from jax.experimental import pallas as pl
from jax.experimental.pallas import tpu as pltpu
from jax.sharding import PartitionSpec as P

BF16 = jnp.bfloat16
F32 = jnp.float32
OFFSETS = (0, 1, -2, 3, 4)
LANES = 128


def params():
    return pltpu.CompilerParams(vmem_limit_bytes=24 * 1024 * 1024)


def cost(flops, size):
    return pl.CostEstimate(flops=flops, bytes_accessed=size, transcendentals=0)


def tile_at(panel, l, offset):
    return pl.multiple_of(lax.rem(2 * panel + l + offset + 8, 8) * LANES, LANES)


def swap_blocks(x):
    lane = lax.broadcasted_iota(jnp.int32, (64, LANES), 1)
    top, bottom = x[:64], x[64:]
    low = lane < 64
    upper = jnp.where(low, top, pltpu.roll(bottom, 64, 1))
    lower = jnp.where(low, pltpu.roll(top, 64, 1), bottom)
    even = (lane[:32] & 32) == 0
    parts = []
    for half in (upper, lower):
        first, second = half[:32], half[32:]
        parts.append(jnp.where(even, first, pltpu.roll(second, 32, 1)))
        parts.append(jnp.where(even, pltpu.roll(first, 96, 1), second))
    return jnp.concatenate(parts, axis=0)


def contract_last(a, b):
    return lax.dot_general(a, b, (((1,), (1,)), ((), ())), preferred_element_type=F32)


def interleave(both):
    return [jnp.concatenate([both[0][:, r : r + 4], both[1][:, r : r + 4]], axis=1) for r in (0, 4)]


def pack_kernel(eta_ref, gamma_ref, out_ref, held, sems):
    panel = lax.axis_index("panel")
    copies = {}
    for arr, ref in enumerate((eta_ref, gamma_ref)):
        for l in range(2):
            for ch in range(2):
                rows = slice(l * 128, (l + 1) * 128)
                copy = pltpu.make_async_copy(ref.at[ch, rows], held.at[arr, ch, rows], sems.at[arr, l, ch])
                copy.start()
                copies[arr, l, ch] = copy
    for arr in range(2):
        for l in range(2):
            for ch in range(2):
                copies[arr, l, ch].wait()
            pieces = []
            for offset in OFFSETS:
                column = tile_at(panel, l, offset)
                pieces += interleave([swap_blocks(held[arr, ch, l * 128 : (l + 1) * 128, pl.ds(column, LANES)].astype(F32)).reshape(16, 8, LANES) for ch in range(2)])
            start = arr * 32 + l * 16
            out_ref[start : start + 16] = jnp.concatenate(pieces, axis=1).astype(BF16)


def spread_kernel(forward_ref, back_ref, weight_ref, forward_out, back_out, rows_out):
    panel = lax.axis_index("panel")
    for ch in range(2):
        for j in range(8):
            lane = weight_ref[ch : ch + 1, pl.ds(tile_at(panel, j, 0), LANES)]
            rows_out[ch, j] = jnp.broadcast_to(lane, (128, LANES)).T
    for ref, out in ((forward_ref, forward_out), (back_ref, back_out)):
        shift = 2
        size = 128 << shift
        row = lax.broadcasted_iota(jnp.int32, (size, 128), 0) >> shift
        column = lax.broadcasted_iota(jnp.int32, (size, 128), 1)
        copies = jnp.where(row == column, F32(1.0), F32(0.0)).astype(BF16)
        tall = jnp.dot(copies, ref[...], preferred_element_type=F32).astype(BF16)
        mask = (1 << shift) - 1
        for start in range(0, size, 256):
            wide = contract_last(tall[start : start + 256], copies)
            row = lax.broadcasted_iota(jnp.int32, wide.shape, 0) & mask
            column = lax.broadcasted_iota(jnp.int32, wide.shape, 1) & mask
            out[start : start + 256, :] = jnp.where(row == column, wide, F32(0.0)).astype(BF16)


def recouple_rows(table_ref, in_ref, count):
    value = in_ref[...].astype(F32)
    rhs = jnp.concatenate([value[:, q * 8 : q * 8 + 8].reshape(512, LANES) for q in range(count)], axis=1).astype(BF16)
    mixed = jnp.dot(table_ref[...], rhs, preferred_element_type=F32)
    return [mixed[:, q * LANES : (q + 1) * LANES].reshape(64, 8, LANES) for q in range(count)]


def recouple_kernel(table_ref, in_ref, out_ref):
    pieces = recouple_rows(table_ref, in_ref, 10)
    for ch in range(2):
        rows = [piece[:, ch * 4 : ch * 4 + 4] for piece in pieces]
        out_ref[:, ch * 40 : ch * 40 + 40] = jnp.concatenate(rows, axis=1).astype(BF16)


def tile_of(ref, ch, arr, l, t):
    start = arr * 32 + l * 16
    return ref[start : start + 16].astype(F32)[:, ch * 40 + t * 8 : ch * 40 + t * 8 + 8].reshape(128, LANES)


PLUS = ((1, 1), (0, 3))
MINUS = ((0, 2), (1, 2))
FAR = ((1, 3),)


def mirror_kernel(in_ref, plus_ref, minus_ref, far_ref):
    for ch in range(2):
        for arr in range(2):
            base = (ch * 2 + arr) * 4
            for u, (l, t) in enumerate(PLUS + ((0, 4), (1, 3))):
                plus_ref[base + u] = tile_of(in_ref, ch, arr, l, t).T.astype(BF16)
            for u, (l, t) in enumerate(MINUS):
                minus_ref[base + u] = tile_of(in_ref, ch, arr, l, t).T.astype(BF16)
            for u, (l, t) in enumerate(((1, 3), (1, 4))):
                tile = tile_of(in_ref, ch, arr, l, t)
                minus_ref[base + 2 + u] = (-tile if arr == 0 else tile).astype(BF16)
            far_ref[ch * 2 + arr] = tile_of(in_ref, ch, arr, *FAR[0]).T.astype(BF16)


def product_kernel(in_ref, plus_ref, minus_ref, far_ref, weight_ref, rows_ref, *refs):
    for ch in range(2):
        product_channel(ch, in_ref, plus_ref, minus_ref, far_ref, weight_ref, rows_ref, *refs)


def product_channel(
    ch, in_ref, plus_ref, minus_ref, far_ref, weight_ref, rows_ref, own_ref, plus_out, far_out, minus_out, by_lane, by_row, plain, edge_lane, edge_row, edge_plain
):
    own_ref, plus_out, far_out, minus_out, by_lane, by_row, plain, edge_lane, edge_row, edge_plain = (
        ref.at[ch] for ref in (own_ref, plus_out, far_out, minus_out, by_lane, by_row, plain, edge_lane, edge_row, edge_plain)
    )
    panel = lax.axis_index("panel")
    lanes = [weight_ref[ch : ch + 1, pl.ds(tile_at(panel, j, 0), LANES)] for j in range(4)]
    rows = [rows_ref[ch, j] for j in range(8)]
    for l in range(2):

        def put(arr, offset, value):
            j = (l + offset) % 8
            place = (slice(j * 128, (j + 1) * 128), slice(l * LANES, (l + 1) * LANES))
            if arr == 0:
                by_lane[place] = (value * lanes[l]).astype(BF16)
                by_row[place] = (value * rows[j]).astype(BF16)
            else:
                plain[place] = value.astype(BF16)

        for arr in range(2):
            for t, offset in enumerate(OFFSETS):
                tile = tile_of(in_ref, ch, arr, l, t)
                put(arr, offset, -tile if arr == 0 else tile)
            put(arr, 2, minus_ref[(ch * 2 + arr) * 4 + l].astype(F32))
            if l == 0:
                put(arr, -1, plus_ref[(ch * 2 + arr) * 4].astype(F32))
                put(arr, -3, far_ref[ch * 2 + arr].astype(F32))
            else:
                put(arr, -1, tile_of(in_ref, ch, arr, 0, 1).T)
                put(arr, -3, plus_ref[(ch * 2 + arr) * 4 + 1].astype(F32))
    for arr in range(2):
        for r in range(2):
            for c in range(2):
                ref = plus_ref if c == 0 else minus_ref
                value = ref[(ch * 2 + arr) * 4 + 2 + r].astype(F32)
                place = (slice(r * 128, (r + 1) * 128), slice(c * LANES, (c + 1) * LANES))
                if arr == 0:
                    edge_lane[place] = (value * lanes[2 + c]).astype(BF16)
                    edge_row[place] = (value * rows[6 + r]).astype(BF16)
                else:
                    edge_plain[place] = value.astype(BF16)

    def block(ref, j):
        return ref[j * 256 : (j + 1) * 256]

    def inner(i, j):
        return contract_last(block(by_lane, i), block(plain, j)) + contract_last(block(plain, i), block(by_lane, j))

    def tile(value, i, j):
        return value[i * 128 : (i + 1) * 128, j * 128 : (j + 1) * 128]

    diagonal = contract_first(by_row[...], plain[...]) + contract_first(plain[...], by_row[...])
    for (l, t), (i, j) in (((0, 0), (0, 0)), ((0, 1), (0, 1)), ((1, 0), (1, 1))):
        own_ref[l, t] = -tile(diagonal, i, j)
    ahead = inner(0, 1) - contract_first(block(by_row, 3), edge_plain[...]) - contract_first(block(plain, 3), edge_row[...])
    own_ref[0, 3] = tile(ahead, 0, 1)
    own_ref[1, 1] = tile(ahead, 1, 0)
    plus_out[0] = tile(ahead, 0, 0).astype(BF16)
    plus_out[1] = tile(ahead, 1, 1).astype(BF16)
    behind = inner(3, 0)
    behind += jnp.dot(edge_lane[...], block(plain, 1), preferred_element_type=F32)
    behind -= jnp.dot(edge_plain[...], block(by_row, 1), preferred_element_type=F32)
    own_ref[0, 2] = tile(behind, 0, 0)
    own_ref[1, 2] = tile(behind, 1, 1)
    minus_out[0] = tile(behind, 0, 1).astype(BF16)
    minus_out[1] = tile(behind, 1, 0).astype(BF16)
    across = inner(0, 2)
    for (l, t), (i, j) in ACROSS:
        own_ref[l, t] = tile(across, i, j)
    for ref, start, value in ((far_out, 0, inner(2, 0)), (minus_out, 2, inner(3, 1)), (plus_out, 2, inner(1, 3))):
        for u, (held, (i, j)) in enumerate(ACROSS):
            ref[start + u] = tile(value, i, j).astype(BF16)


ACROSS = (((0, 4), (0, 0)), ((1, 3), (1, 0)), ((1, 4), (1, 1)))


def total(own_ref, plus_ref, far_ref, minus_ref, l, t):
    value = own_ref[l, t]
    if t == 2:
        return (value + plus_ref[l].astype(F32)).T
    if (l, t) in ((0, 3), (1, 1)):
        return value + minus_ref[l].astype(F32)
    for u, (held, _) in enumerate(ACROSS):
        if held == (l, t):
            near = plus_ref[2 + u].astype(F32) + minus_ref[2 + u].astype(F32)
            return value + far_ref[u].astype(F32) + near
    return value


def sum_kernel(own_ref, plus_ref, far_ref, minus_ref, out_ref):
    refs = (own_ref, plus_ref, far_ref, minus_ref)
    for l in range(2):
        low, high = [], []
        for t in range(5):
            pieces = interleave([swap_blocks(total(*(ref.at[ch] for ref in refs), l, t)).reshape(16, 8, LANES) for ch in range(2)])
            low.append(pieces[0])
            high.append(pieces[1])
        out_ref[l * 32 : l * 32 + 16] = jnp.concatenate(low, axis=1).astype(BF16)
        out_ref[l * 32 + 16 : l * 32 + 32] = jnp.concatenate(high, axis=1).astype(BF16)


def recouple_back_kernel(table_ref, in_ref, out_ref):
    out_ref[...] = jnp.concatenate(recouple_rows(table_ref, in_ref, 5), axis=1).astype(BF16)


def back_tile(ref, l, t, ch):
    low = ref[l * 32 : l * 32 + 16].astype(F32)[:, t * 8 + ch * 4 : t * 8 + ch * 4 + 4]
    high = ref[l * 32 + 16 : l * 32 + 32].astype(F32)[:, t * 8 + ch * 4 : t * 8 + ch * 4 + 4]
    return jnp.concatenate([low, high], axis=1).reshape(128, LANES)


def back_mirror_kernel(in_ref, pp_ref, plus_ref, minus_ref, far_ref):
    for ch in range(2):
        for ref, held in ((plus_ref, PLUS), (minus_ref, MINUS), (far_ref, FAR)):
            for u, (l, t) in enumerate(held):
                ref[ch * len(held) + u] = (pp_ref[l, t, ch].T + back_tile(in_ref, l, t, ch)).astype(BF16)


def finish_kernel(in_ref, plus_ref, minus_ref, far_ref, pp_ref, out_ref):
    panel = lax.axis_index("panel")
    for ch in range(2):
        for l in range(2):

            def put(offset, value):
                out_ref[ch, l * 128 : (l + 1) * 128, pl.ds(tile_at(panel, l, offset), LANES)] = value.astype(BF16)

            for t, offset in enumerate(OFFSETS):
                put(offset, pp_ref[l, t, ch] + back_tile(in_ref, l, t, ch).T)
            put(2, minus_ref[ch * 2 + l])
            if l == 0:
                put(-1, plus_ref[ch * 2])
                put(-3, far_ref[ch])
            else:
                put(-1, pp_ref[0, 1, ch].T + back_tile(in_ref, 0, 1, ch))
                put(-3, plus_ref[ch * 2 + 1])


def contract_first(a, b):
    return lax.dot_general(a, b, (((0,), (0,)), ((), ())), preferred_element_type=F32)


def pair_kernel(eta_ref, gamma_ref, weight_ref, own_ref, plus_ref, far_ref, minus_ref, scaled, plain):
    panel = lax.axis_index("panel")
    for ch in range(2):
        for l in range(2):
            row = weight_ref[ch : ch + 1, pl.ds(tile_at(panel, l, 0), LANES)]
            weight = jnp.broadcast_to(row, (128, LANES)).T
            rows = slice(l * 128, (l + 1) * 128)
            for j in range(8):
                source = pl.ds(tile_at(panel, j, 0), LANES)
                columns = slice(j * LANES, (j + 1) * LANES)
                scaled[ch, rows, columns] = (eta_ref[ch, rows, source].astype(F32) * weight).astype(BF16)
                plain[ch, rows, columns] = gamma_ref[ch, rows, source]
        for owner, ref in enumerate((own_ref, plus_ref, far_ref, minus_ref)):
            columns = slice(owner * 256, (owner + 1) * 256)
            total = contract_first(scaled[ch, :, columns], plain[ch]) + contract_first(plain[ch, :, columns], scaled[ch])
            for l in range(2):
                for t, offset in enumerate(OFFSETS):
                    column = (2 * owner + l + offset) % 8 * LANES
                    ref[l, t, ch] = -total[l * 128 : (l + 1) * 128, column : column + LANES].astype(BF16)


def pair_sum_kernel(own_ref, plus_ref, far_ref, minus_ref, out_ref):
    for l in range(2):
        for t in range(5):
            for ch in range(2):
                parts = [ref[l, t, ch].astype(F32) for ref in (own_ref, plus_ref, far_ref, minus_ref)]
                out_ref[l, t, ch] = (parts[0] + parts[1]) + (parts[2] + parts[3])


def call(kernel, shapes, args, flops=0, scratch=(), name=None, dtype=BF16, space=None):
    single = not isinstance(shapes, list)
    outs = [shapes] if single else shapes
    types = dtype if isinstance(dtype, list) else [dtype] * len(outs)
    shaped = [jax.ShapeDtypeStruct(s, d) for s, d in zip(outs, types)]
    size = sum(a.size * a.dtype.itemsize for a in [*args, *shaped])
    return pl.pallas_call(
        kernel,
        out_shape=shaped[0] if single else shaped,
        in_specs=[pl.BlockSpec(memory_space=space or pltpu.VMEM)] * len(args),
        scratch_shapes=list(scratch),
        compiler_params=params(),
        cost_estimate=cost(flops, size),
        name=name,
    )(*args)


def exchange(operand, axis):
    return lax.all_to_all(operand, axis, split_axis=0, concat_axis=0, tiled=True)


def step(value, by):
    return lax.ppermute(value, "panel", [(i, (i + by) % 4) for i in range(4)])


def mirror(plus, minus, far):
    return step(plus, 1), step(minus, 3), step(far, 2)


def shards(eta, gamma, pp_weight, cc_weight, live_pairs, forward_table, back_table):
    positions = lax.broadcasted_iota(jnp.int32, pp_weight.shape, 1)
    weight_pp = jnp.where(positions < live_pairs[:, None], pp_weight, F32(0.0))
    packed = call(
        pack_kernel,
        (64, 80, LANES),
        (eta, gamma),
        scratch=[pltpu.VMEM((2, 2, 256, 1024), BF16), pltpu.SemaphoreType.DMA((2, 2, 2))],
        name="pack",
        space=pltpu.HBM,
    )
    forward_wide, back_wide, weight_rows = call(
        spread_kernel,
        [(512, 512), (512, 512), (2, 8, 128, LANES)],
        (forward_table, back_table, cc_weight),
        flops=300_000_000,
        name="spread",
        dtype=[BF16, BF16, F32],
    )
    packed = exchange(packed, "chan")
    pp_own, *pp = call(
        pair_kernel,
        [(2, 5, 2, 128, LANES)] * 4,
        (eta, gamma, weight_pp),
        flops=2_200_000_000,
        scratch=[pltpu.VMEM((2, 256, 1024), BF16)] * 2,
        name="pair",
    )
    pp_plus, pp_minus = step(pp[0], 1), step(pp[2], 3)
    packed, pp_own, pp_far, pp_plus, pp_minus = lax.optimization_barrier((packed, pp_own, pp[1], pp_plus, pp_minus))
    mixed = call(recouple_kernel, (64, 80, LANES), (forward_wide, packed), flops=700_000_000, name="recouple")
    mixed = exchange(mixed, "chan")
    pp_far = step(pp_far, 2)
    pp_part = call(pair_sum_kernel, (2, 5, 2, 128, LANES), (pp_own, pp_plus, pp_far, pp_minus), name="pair_sum", dtype=F32)
    mixed, pp_part = lax.optimization_barrier((mixed, pp_part))
    sends = call(mirror_kernel, [(16, 128, LANES), (16, 128, LANES), (4, 128, LANES)], (mixed,), name="mirror")
    received = mirror(*sends)
    own, *partial = call(
        product_kernel,
        [(2, 2, 5, 128, LANES), (2, 5, 128, LANES), (2, 3, 128, LANES), (2, 5, 128, LANES)],
        (mixed, *received, cc_weight, weight_rows),
        flops=1_400_000_000,
        scratch=[pltpu.VMEM((2, 1024, 256), BF16)] * 3 + [pltpu.VMEM((2, 256, 256), BF16)] * 3,
        name="product",
        dtype=[F32, BF16, BF16, BF16],
    )
    plus, minus, far = mirror(partial[0], partial[2], partial[1])
    part = call(sum_kernel, (64, 40, LANES), (own, plus, far, minus), name="sum")
    part = exchange(part, "chan")
    part = call(recouple_back_kernel, (64, 40, LANES), (back_wide, part), flops=400_000_000, name="recouple_back")
    part = exchange(part, "chan")
    back_sends = call(back_mirror_kernel, [(4, 128, LANES), (4, 128, LANES), (2, 128, LANES)], (part, pp_part), name="back_mirror")
    back_received = mirror(*back_sends)
    return call(finish_kernel, (2, 256, 1024), (part, *back_received, pp_part), name="finish")


def solution(mesh):
    in_specs = (
        P("chan", "panel", None),
        P("chan", "panel", None),
        P("chan", None),
        P("chan", None),
        P("chan"),
        P(),
        P(),
    )
    out_specs = P("chan", "panel", None)
    return jax.shard_map(shards, mesh=mesh, in_specs=in_specs, out_specs=out_specs, check_vma=False)
```

```python
import jax
import jax.numpy as jnp
from jax import lax
from jax.experimental import pallas as pl
from jax.experimental.pallas import tpu as pltpu
from jax.sharding import PartitionSpec as P

BF16 = jnp.bfloat16
F32 = jnp.float32
OFFSETS = (0, 1, -2, 3, 4)
LANES = 128


def params(mib=24):
    return pltpu.CompilerParams(vmem_limit_bytes=mib * 1024 * 1024)


def cost(flops, size):
    return pl.CostEstimate(flops=flops, bytes_accessed=size, transcendentals=0)


def tile_at(panel, l, offset):
    return pl.multiple_of(lax.rem(2 * panel + l + offset + 8, 8) * LANES, LANES)


def swap_blocks(x):
    lane = lax.broadcasted_iota(jnp.int32, (64, LANES), 1)
    top, bottom = x[:64], x[64:]
    low = lane < 64
    upper = jnp.where(low, top, pltpu.roll(bottom, 64, 1))
    lower = jnp.where(low, pltpu.roll(top, 64, 1), bottom)
    even = (lane[:32] & 32) == 0
    parts = []
    for half in (upper, lower):
        first, second = half[:32], half[32:]
        parts.append(jnp.where(even, first, pltpu.roll(second, 32, 1)))
        parts.append(jnp.where(even, pltpu.roll(first, 96, 1), second))
    return jnp.concatenate(parts, axis=0)


def contract_last(a, b):
    return lax.dot_general(a, b, (((1,), (1,)), ((), ())), preferred_element_type=F32)


def interleave(both):
    return [jnp.concatenate([both[0][:, r : r + 4], both[1][:, r : r + 4]], axis=1) for r in (0, 4)]


def pack_kernel(eta_ref, gamma_ref, out_ref, held, sems):
    panel = lax.axis_index("panel")
    either = jnp.where(panel < 2, 0, 1)
    row = lax.broadcasted_iota(jnp.int32, (128, LANES), 0)
    column = lax.broadcasted_iota(jnp.int32, (128, LANES), 1)
    source = (("both", 0, 0, 0, either, 0, 1, 1), (1, "both", 0, 0, 1, either, 1, 1))
    copies = {}
    for l in range(2):
        for ch in range(2):
            for arr, ref in enumerate((eta_ref, gamma_ref)):
                rows = slice(l * 128, (l + 1) * 128)
                copy = pltpu.make_async_copy(ref.at[ch, rows], held.at[arr, ch, rows], sems.at[l, ch, arr])
                copy.start()
                copies[l, ch, arr] = copy

    def tile(ch, l, j):
        def read(arr):
            return held[arr, ch, l * 128 : (l + 1) * 128, pl.ds(tile_at(panel, j, 0), LANES)]

        kind = source[l][j]
        value = jnp.where(row < column, read(0), read(1)) if kind == "both" else read(kind)
        return swap_blocks(value).astype(F32).reshape(16, 8, LANES)

    for l in range(2):
        for ch in range(2):
            for arr in range(2):
                copies[l, ch, arr].wait()
        for part in range(2):
            pieces = []
            for j in range(part * 4, part * 4 + 4):
                pieces += interleave([tile(ch, l, j) for ch in range(2)])
            start = part * 32 + l * 16
            out_ref[start : start + 16] = jnp.concatenate(pieces, axis=1).astype(BF16)


def spread_kernel(forward_ref, back_ref, weight_ref, forward_out, back_out, rows_out):
    panel = lax.axis_index("panel")
    for ch in range(2):
        for j in range(8):
            lane = weight_ref[ch : ch + 1, pl.ds(tile_at(panel, j, 0), LANES)]
            rows_out[ch, j] = jnp.broadcast_to(lane, (128, LANES)).T
    for ref, out in ((forward_ref, forward_out), (back_ref, back_out)):
        shift = 2
        size = 128 << shift
        row = lax.broadcasted_iota(jnp.int32, (size, 128), 0) >> shift
        column = lax.broadcasted_iota(jnp.int32, (size, 128), 1)
        copies = jnp.where(row == column, F32(1.0), F32(0.0)).astype(BF16)
        tall = jnp.dot(copies, ref[...], preferred_element_type=F32).astype(BF16)
        mask = (1 << shift) - 1
        for start in range(0, size, 256):
            wide = contract_last(tall[start : start + 256], copies)
            row = lax.broadcasted_iota(jnp.int32, wide.shape, 0) & mask
            column = lax.broadcasted_iota(jnp.int32, wide.shape, 1) & mask
            out[start : start + 256, :] = jnp.where(row == column, wide, F32(0.0)).astype(BF16)


def recouple_rows(table_ref, in_ref, count):
    value = in_ref[...].astype(F32)
    rhs = jnp.concatenate([value[:, q * 8 : q * 8 + 8].reshape(512, LANES) for q in range(count)], axis=1).astype(BF16)
    mixed = jnp.dot(table_ref[...], rhs, preferred_element_type=F32)
    return [mixed[:, q * LANES : (q + 1) * LANES].reshape(64, 8, LANES) for q in range(count)]


def recouple_kernel(table_ref, in_ref, out_ref):
    pieces = recouple_rows(table_ref, in_ref, 8)
    for ch in range(2):
        rows = [piece[:, ch * 4 : ch * 4 + 4] for piece in pieces]
        out_ref[:, ch * 32 : ch * 32 + 32] = jnp.concatenate(rows, axis=1).astype(BF16)


def tile_of(ref, ch, l, j):
    start = j // 4 * 32 + l * 16
    return ref[start : start + 16].astype(F32)[:, ch * 32 + j % 4 * 8 : ch * 32 + j % 4 * 8 + 8].reshape(128, LANES)


PLUS = ((1, 1), (0, 3))
MINUS = ((0, 2), (1, 2))
FAR = ((1, 3),)


def mirror_kernel(in_ref, plus_ref, minus_ref, far_ref):
    for ch in range(2):
        for l in range(2):
            for k in range(2):
                plus_ref[ch, 0, l, k] = tile_of(in_ref, ch, l, 2 + k).astype(BF16)
                minus_ref[ch, 0, l, k] = tile_of(in_ref, ch, l, 6 + k).astype(BF16)
                across = tile_of(in_ref, ch, l, 4 + k).astype(BF16)
                plus_ref[ch, 1, l, k] = across
                minus_ref[ch, 1, l, k] = across
                far_ref[ch, l, k] = across


def product_kernel(in_ref, plus_ref, minus_ref, far_ref, weight_ref, rows_ref, *refs):
    for ch in range(2):
        product_channel(ch, in_ref, plus_ref, minus_ref, far_ref, weight_ref, rows_ref, *refs)


def product_channel(
    ch, in_ref, plus_ref, minus_ref, far_ref, weight_ref, rows_ref, own_ref, plus_out, far_out, minus_out, by_lane, by_row, plain, edge_lane, edge_row, edge_plain
):
    own_ref, plus_out, far_out, minus_out, by_lane, by_row, plain, edge_lane, edge_row, edge_plain = (
        ref.at[ch] for ref in (own_ref, plus_out, far_out, minus_out, by_lane, by_row, plain, edge_lane, edge_row, edge_plain)
    )
    panel = lax.axis_index("panel")
    lanes = [weight_ref[ch : ch + 1, pl.ds(tile_at(panel, j, 0), LANES)] for j in range(4)]
    rows = [rows_ref[ch, j] for j in range(8)]

    def held(l, j):
        return tile_of(in_ref, ch, l, j)

    def plus(part, i, k):
        return plus_ref[ch, part, i, k].astype(F32)

    def minus(part, i, k):
        return minus_ref[ch, part, i, k].astype(F32)

    def far(i, k):
        return far_ref[ch, i, k].astype(F32)

    def put(j, l, eta, gamma):
        place = (slice(j * 128, (j + 1) * 128), slice(l * LANES, (l + 1) * LANES))
        by_lane[place] = (eta * lanes[l]).astype(BF16)
        by_row[place] = (eta * rows[j]).astype(BF16)
        plain[place] = gamma.astype(BF16)

    def put_edge(i, k, eta, gamma):
        place = (slice(i * 128, (i + 1) * 128), slice(k * LANES, (k + 1) * LANES))
        edge_lane[place] = (eta * lanes[2 + k]).astype(BF16)
        edge_row[place] = (eta * rows[6 + i]).astype(BF16)
        edge_plain[place] = gamma.astype(BF16)

    row = lax.broadcasted_iota(jnp.int32, (128, LANES), 0)
    column = lax.broadcasted_iota(jnp.int32, (128, LANES), 1)
    row_block, column_block = row >> 5, column >> 5
    first = (row_block > column_block) | ((row_block == column_block) & (row < column))
    for l in range(2):
        value = held(l, l)
        mirrored = value.T
        put(l, l, jnp.where(row == column, F32(0.0), jnp.where(first, -value, mirrored)), jnp.where(first, mirrored, value))
        for k in range(2):
            put(2 + k, l, -held(l, 2 + k), minus(0, k, l).T)
            put(6 + k, l, plus(0, k, l).T, held(l, 6 + k))
        value, mirrored = held(l, 4 + l), far(l, l).T
        put(4 + l, l, jnp.where(panel < 2, -value, mirrored), jnp.where(panel < 2, mirrored, value))
        straight, mirrored = minus(1, l, l), plus(1, l, l).T
        before = lax.rem(panel + 3, 4) < 2
        put_edge(l, l, jnp.where(before, mirrored, -straight), jnp.where(before, straight, mirrored))
    put(1, 0, -held(0, 1), held(1, 0).T)
    put(0, 1, held(0, 1).T, held(1, 0))
    put(5, 0, -held(0, 5), far(1, 0).T)
    put(4, 1, far(0, 1).T, held(1, 4))
    put_edge(0, 1, plus(1, 0, 1).T, minus(1, 1, 0))
    put_edge(1, 0, -minus(1, 0, 1), plus(1, 1, 0).T)

    def block(ref, j):
        return ref[j * 256 : (j + 1) * 256]

    def inner(i, j):
        return contract_last(block(by_lane, i), block(plain, j)) + contract_last(block(plain, i), block(by_lane, j))

    def tile(value, i, j):
        return value[i * 128 : (i + 1) * 128, j * 128 : (j + 1) * 128]

    diagonal = contract_first(by_row[...], plain[...]) + contract_first(plain[...], by_row[...])
    for (l, t), (i, j) in (((0, 0), (0, 0)), ((0, 1), (0, 1)), ((1, 0), (1, 1))):
        own_ref[l, t] = -tile(diagonal, i, j)
    ahead = inner(0, 1) - contract_first(block(by_row, 3), edge_plain[...]) - contract_first(block(plain, 3), edge_row[...])
    own_ref[0, 3] = tile(ahead, 0, 1)
    own_ref[1, 1] = tile(ahead, 1, 0)
    plus_out[0] = tile(ahead, 0, 0).astype(BF16)
    plus_out[1] = tile(ahead, 1, 1).astype(BF16)
    behind = inner(3, 0)
    behind += jnp.dot(edge_lane[...], block(plain, 1), preferred_element_type=F32)
    behind -= jnp.dot(edge_plain[...], block(by_row, 1), preferred_element_type=F32)
    own_ref[0, 2] = tile(behind, 0, 0)
    own_ref[1, 2] = tile(behind, 1, 1)
    minus_out[0] = tile(behind, 0, 1).astype(BF16)
    minus_out[1] = tile(behind, 1, 0).astype(BF16)
    across = inner(0, 2)
    for (l, t), (i, j) in ACROSS:
        own_ref[l, t] = tile(across, i, j)
    for ref, start, value in ((far_out, 0, inner(2, 0)), (minus_out, 2, inner(3, 1)), (plus_out, 2, inner(1, 3))):
        for u, (held, (i, j)) in enumerate(ACROSS):
            ref[start + u] = tile(value, i, j).astype(BF16)


ACROSS = (((0, 4), (0, 0)), ((1, 3), (1, 0)), ((1, 4), (1, 1)))


def total(own_ref, plus_ref, far_ref, minus_ref, l, t):
    value = own_ref[l, t]
    if t == 2:
        return (value + plus_ref[l].astype(F32)).T
    if (l, t) in ((0, 3), (1, 1)):
        return value + minus_ref[l].astype(F32)
    for u, (held, _) in enumerate(ACROSS):
        if held == (l, t):
            near = plus_ref[2 + u].astype(F32) + minus_ref[2 + u].astype(F32)
            return value + far_ref[u].astype(F32) + near
    return value


def sum_kernel(own_ref, plus_ref, far_ref, minus_ref, out_ref):
    refs = (own_ref, plus_ref, far_ref, minus_ref)
    for l in range(2):
        low, high = [], []
        for t in range(5):
            pieces = interleave([swap_blocks(total(*(ref.at[ch] for ref in refs), l, t)).reshape(16, 8, LANES) for ch in range(2)])
            low.append(pieces[0])
            high.append(pieces[1])
        out_ref[l * 32 : l * 32 + 16] = jnp.concatenate(low, axis=1).astype(BF16)
        out_ref[l * 32 + 16 : l * 32 + 32] = jnp.concatenate(high, axis=1).astype(BF16)


def recouple_back_kernel(table_ref, in_ref, out_ref):
    out_ref[...] = jnp.concatenate(recouple_rows(table_ref, in_ref, 5), axis=1).astype(BF16)


def back_tile(ref, l, t, ch):
    low = ref[l * 32 : l * 32 + 16].astype(F32)[:, t * 8 + ch * 4 : t * 8 + ch * 4 + 4]
    high = ref[l * 32 + 16 : l * 32 + 32].astype(F32)[:, t * 8 + ch * 4 : t * 8 + ch * 4 + 4]
    return jnp.concatenate([low, high], axis=1).reshape(128, LANES)


def back_mirror_kernel(in_ref, pp_ref, plus_ref, minus_ref, far_ref):
    for ch in range(2):
        for ref, held in ((plus_ref, PLUS), (minus_ref, MINUS), (far_ref, FAR)):
            for u, (l, t) in enumerate(held):
                ref[ch * len(held) + u] = (pp_ref[l, t, ch].T + back_tile(in_ref, l, t, ch)).astype(BF16)


def finish_kernel(in_ref, plus_ref, minus_ref, far_ref, pp_ref, out_ref):
    panel = lax.axis_index("panel")
    for ch in range(2):
        for l in range(2):

            def put(offset, value):
                out_ref[ch, l * 128 : (l + 1) * 128, pl.ds(tile_at(panel, l, offset), LANES)] = value.astype(BF16)

            for t, offset in enumerate(OFFSETS):
                put(offset, pp_ref[l, t, ch] + back_tile(in_ref, l, t, ch).T)
            put(2, minus_ref[ch * 2 + l])
            if l == 0:
                put(-1, plus_ref[ch * 2])
                put(-3, far_ref[ch])
            else:
                put(-1, pp_ref[0, 1, ch].T + back_tile(in_ref, 0, 1, ch))
                put(-3, plus_ref[ch * 2 + 1])


def contract_first(a, b):
    return lax.dot_general(a, b, (((0,), (0,)), ((), ())), preferred_element_type=F32)


def pair_kernel(eta_ref, gamma_ref, weight_ref, own_ref, plus_ref, far_ref, minus_ref, scaled, plain):
    panel = lax.axis_index("panel")
    for ch in range(2):
        for l in range(2):
            row = weight_ref[ch : ch + 1, pl.ds(tile_at(panel, l, 0), LANES)]
            weight = jnp.broadcast_to(row, (128, LANES)).T
            rows = slice(l * 128, (l + 1) * 128)
            for j in range(8):
                source = pl.ds(tile_at(panel, j, 0), LANES)
                columns = slice(j * LANES, (j + 1) * LANES)
                scaled[ch, rows, columns] = (eta_ref[ch, rows, source].astype(F32) * weight).astype(BF16)
                plain[ch, rows, columns] = gamma_ref[ch, rows, source]
        for owner, ref in enumerate((own_ref, plus_ref, far_ref, minus_ref)):
            columns = slice(owner * 256, (owner + 1) * 256)
            total = contract_first(scaled[ch, :, columns], plain[ch]) + contract_first(plain[ch, :, columns], scaled[ch])
            for l in range(2):
                for t, offset in enumerate(OFFSETS):
                    column = (2 * owner + l + offset) % 8 * LANES
                    ref[l, t, ch] = -total[l * 128 : (l + 1) * 128, column : column + LANES].astype(BF16)


def pair_sum_kernel(own_ref, plus_ref, far_ref, minus_ref, out_ref):
    for l in range(2):
        for t in range(5):
            for ch in range(2):
                parts = [ref[l, t, ch].astype(F32) for ref in (own_ref, plus_ref, far_ref, minus_ref)]
                out_ref[l, t, ch] = (parts[0] + parts[1]) + (parts[2] + parts[3])


def call(kernel, shapes, args, flops=0, scratch=(), name=None, dtype=BF16, space=None):
    single = not isinstance(shapes, list)
    outs = [shapes] if single else shapes
    types = dtype if isinstance(dtype, list) else [dtype] * len(outs)
    shaped = [jax.ShapeDtypeStruct(s, d) for s, d in zip(outs, types)]
    size = sum(a.size * a.dtype.itemsize for a in [*args, *shaped])
    return pl.pallas_call(
        kernel,
        out_shape=shaped[0] if single else shaped,
        in_specs=[pl.BlockSpec(memory_space=space or pltpu.VMEM)] * len(args),
        scratch_shapes=list(scratch),
        compiler_params=params(60 if space else 24),
        cost_estimate=cost(flops, size),
        name=name,
    )(*args)


def exchange(operand, axis):
    return lax.all_to_all(operand, axis, split_axis=0, concat_axis=0, tiled=True)


def step(value, by):
    return lax.ppermute(value, "panel", [(i, (i + by) % 4) for i in range(4)])


def mirror(plus, minus, far):
    return step(plus, 1), step(minus, 3), step(far, 2)


def shards(eta, gamma, pp_weight, cc_weight, live_pairs, forward_table, back_table):
    positions = lax.broadcasted_iota(jnp.int32, pp_weight.shape, 1)
    weight_pp = jnp.where(positions < live_pairs[:, None], pp_weight, F32(0.0))
    packed = call(
        pack_kernel,
        (64, 64, LANES),
        (eta, gamma),
        scratch=[pltpu.VMEM((2, 2, 256, 1024), BF16), pltpu.SemaphoreType.DMA((2, 2, 2))],
        name="pack",
        space=pltpu.HBM,
    )
    forward_wide, back_wide, weight_rows = call(
        spread_kernel,
        [(512, 512), (512, 512), (2, 8, 128, LANES)],
        (forward_table, back_table, cc_weight),
        flops=300_000_000,
        name="spread",
        dtype=[BF16, BF16, F32],
    )
    packed = exchange(packed, "chan")
    pp_own, *pp = call(
        pair_kernel,
        [(2, 5, 2, 128, LANES)] * 4,
        (eta, gamma, weight_pp),
        flops=2_200_000_000,
        scratch=[pltpu.VMEM((2, 256, 1024), BF16)] * 2,
        name="pair",
    )
    pp_plus, pp_minus = step(pp[0], 1), step(pp[2], 3)
    packed, pp_own, pp_far, pp_plus, pp_minus = lax.optimization_barrier((packed, pp_own, pp[1], pp_plus, pp_minus))
    mixed = call(recouple_kernel, (64, 64, LANES), (forward_wide, packed), flops=700_000_000, name="recouple")
    mixed = exchange(mixed, "chan")
    pp_far = step(pp_far, 2)
    pp_part = call(pair_sum_kernel, (2, 5, 2, 128, LANES), (pp_own, pp_plus, pp_far, pp_minus), name="pair_sum", dtype=F32)
    mixed, pp_part = lax.optimization_barrier((mixed, pp_part))
    sends = call(mirror_kernel, [(2, 2, 2, 2, 128, LANES), (2, 2, 2, 2, 128, LANES), (2, 2, 2, 128, LANES)], (mixed,), name="mirror")
    received = mirror(*sends)
    own, *partial = call(
        product_kernel,
        [(2, 2, 5, 128, LANES), (2, 5, 128, LANES), (2, 3, 128, LANES), (2, 5, 128, LANES)],
        (mixed, *received, cc_weight, weight_rows),
        flops=1_400_000_000,
        scratch=[pltpu.VMEM((2, 1024, 256), BF16)] * 3 + [pltpu.VMEM((2, 256, 256), BF16)] * 3,
        name="product",
        dtype=[F32, BF16, BF16, BF16],
    )
    plus, minus, far = mirror(partial[0], partial[2], partial[1])
    part = call(sum_kernel, (64, 40, LANES), (own, plus, far, minus), name="sum")
    part = exchange(part, "chan")
    part = call(recouple_back_kernel, (64, 40, LANES), (back_wide, part), flops=400_000_000, name="recouple_back")
    part = exchange(part, "chan")
    back_sends = call(back_mirror_kernel, [(4, 128, LANES), (4, 128, LANES), (2, 128, LANES)], (part, pp_part), name="back_mirror")
    back_received = mirror(*back_sends)
    return call(finish_kernel, (2, 256, 1024), (part, *back_received, pp_part), name="finish")


def solution(mesh):
    in_specs = (
        P("chan", "panel", None),
        P("chan", "panel", None),
        P("chan", None),
        P("chan", None),
        P("chan"),
        P(),
        P(),
    )
    out_specs = P("chan", "panel", None)
    return jax.shard_map(shards, mesh=mesh, in_specs=in_specs, out_specs=out_specs, check_vma=False)
```

```python
import jax
import jax.numpy as jnp
from jax import lax
from jax.experimental import pallas as pl
from jax.experimental.pallas import tpu as pltpu
from jax.sharding import PartitionSpec as P

BF16 = jnp.bfloat16
F32 = jnp.float32
OFFSETS = (0, 1, -2, 3, 4)
LANES = 128


def params(mib=24):
    return pltpu.CompilerParams(vmem_limit_bytes=mib * 1024 * 1024)


def cost(flops, size):
    return pl.CostEstimate(flops=flops, bytes_accessed=size, transcendentals=0)


def tile_at(panel, l, offset):
    return pl.multiple_of(lax.rem(2 * panel + l + offset + 8, 8) * LANES, LANES)


def swap_blocks(x):
    lane = lax.broadcasted_iota(jnp.int32, (64, LANES), 1)
    top, bottom = x[:64], x[64:]
    low = lane < 64
    upper = jnp.where(low, top, pltpu.roll(bottom, 64, 1))
    lower = jnp.where(low, pltpu.roll(top, 64, 1), bottom)
    even = (lane[:32] & 32) == 0
    parts = []
    for half in (upper, lower):
        first, second = half[:32], half[32:]
        parts.append(jnp.where(even, first, pltpu.roll(second, 32, 1)))
        parts.append(jnp.where(even, pltpu.roll(first, 96, 1), second))
    return jnp.concatenate(parts, axis=0)


def contract_last(a, b):
    return lax.dot_general(a, b, (((1,), (1,)), ((), ())), preferred_element_type=F32)


def interleave(both):
    return [jnp.concatenate([both[0][:, r : r + 4], both[1][:, r : r + 4]], axis=1) for r in (0, 4)]


SOURCE = ((2, 0, 0, 0, 3, 0, 1, 1), (1, 2, 0, 0, 1, 3, 1, 1))


def pack_kernel(eta_ref, gamma_ref, out_ref, held, sems):
    panel = lax.axis_index("panel")
    either = jnp.where(panel < 2, 0, 1)
    row = lax.broadcasted_iota(jnp.int32, (128, LANES), 0)
    column = lax.broadcasted_iota(jnp.int32, (128, LANES), 1)
    copies = {}
    for l in range(2):
        for ch in range(2):
            for arr, ref in enumerate((eta_ref, gamma_ref)):
                rows = slice(l * 128, (l + 1) * 128)
                copy = pltpu.make_async_copy(ref.at[ch, rows], held.at[arr, ch, rows], sems.at[l, ch, arr])
                copy.start()
                copies[l, ch, arr] = copy

    def tile(ch, l, j):
        def read(arr):
            return held[arr, ch, l * 128 : (l + 1) * 128, pl.ds(tile_at(panel, j, 0), LANES)]

        kind = SOURCE[l][j]
        value = jnp.where(row < column, read(0), read(1)) if kind == 2 else read(either if kind == 3 else kind)
        return swap_blocks(value).astype(F32).reshape(16, 8, LANES)

    for l in range(2):
        for ch in range(2):
            for arr in range(2):
                copies[l, ch, arr].wait()
        for part in range(2):
            pieces = []
            for j in range(part * 4, part * 4 + 4):
                pieces += interleave([tile(ch, l, j) for ch in range(2)])
            start = part * 32 + l * 16
            out_ref[start : start + 16] = jnp.concatenate(pieces, axis=1).astype(BF16)


def spread_kernel(forward_ref, back_ref, forward_out, back_out):
    for ref, out in ((forward_ref, forward_out), (back_ref, back_out)):
        shift = 2
        size = 128 << shift
        row = lax.broadcasted_iota(jnp.int32, (size, 128), 0) >> shift
        column = lax.broadcasted_iota(jnp.int32, (size, 128), 1)
        copies = jnp.where(row == column, F32(1.0), F32(0.0)).astype(BF16)
        tall = jnp.dot(copies, ref[...], preferred_element_type=F32).astype(BF16)
        mask = (1 << shift) - 1
        for start in range(0, size, 256):
            wide = contract_last(tall[start : start + 256], copies)
            row = lax.broadcasted_iota(jnp.int32, wide.shape, 0) & mask
            column = lax.broadcasted_iota(jnp.int32, wide.shape, 1) & mask
            out[start : start + 256, :] = jnp.where(row == column, wide, F32(0.0)).astype(BF16)


def recouple_rows(table_ref, in_ref, count):
    value = in_ref[...].astype(F32)
    rhs = jnp.concatenate([value[:, q * 8 : q * 8 + 8].reshape(512, LANES) for q in range(count)], axis=1).astype(BF16)
    mixed = jnp.dot(table_ref[...], rhs, preferred_element_type=F32)
    return [mixed[:, q * LANES : (q + 1) * LANES].reshape(64, 8, LANES) for q in range(count)]


def recouple_kernel(table_ref, in_ref, out_ref):
    pieces = recouple_rows(table_ref, in_ref, 8)
    for ch in range(2):
        rows = [piece[:, ch * 4 : ch * 4 + 4] for piece in pieces]
        out_ref[:, ch * 32 : ch * 32 + 32] = jnp.concatenate(rows, axis=1).astype(BF16)


PLUS = ((1, 1), (0, 3))
MINUS = ((0, 2), (1, 2))
FAR = ((1, 3),)


def place():
    return lax.rem(lax.axis_index("panel") + 4 - lax.rem(lax.axis_index("chan"), 2), 4)


def send_kernel(in_ref, plus_ref, minus_ref, far_ref):
    here = place()

    def rows(ch):
        return in_ref[:, pl.ds(pl.multiple_of(ch * 32, 32), 32), :]

    plus_ref[...] = rows(jnp.where(here == 1, 1, 0))
    minus_ref[...] = rows(jnp.where(here == 1, 0, 1))
    far_ref[...] = rows(jnp.where(here == 0, 1, 0))


def tile_of(ref, l, j, first=0):
    start = j // 4 * 32 + l * 16
    return ref[start : start + 16, pl.ds(first, 32), :].astype(F32)[:, j % 4 * 8 : j % 4 * 8 + 8].reshape(128, LANES)


def product_kernel(in_ref, plus_ref, minus_ref, far_ref, weight_ref, own_out, plus_out, far_out, minus_out, scaled, plain, forward):
    panel = lax.axis_index("panel")
    own = jnp.where(place() == 2, 1, 0)

    def tile(r, c):
        b, l = divmod(r, 2)
        j = (c - 2 * b) % 8
        if b == 0:
            return tile_of(in_ref, l, j, pl.multiple_of(own * 32, 32))
        return tile_of((minus_ref, far_ref, plus_ref)[b - 1], l, j)

    lanes = []
    for j in range(8):
        columns = pl.ds(tile_at(panel, j, 0), LANES)
        lanes.append(jnp.where(own == 0, weight_ref[0:1, columns], weight_ref[1:2, columns]))

    def put(ref, r, c, value):
        if ref is scaled:
            value = value * lanes[c]
        ref[r * 128 : (r + 1) * 128, c * LANES : (c + 1) * LANES] = value.astype(BF16)

    row = lax.broadcasted_iota(jnp.int32, (128, LANES), 0)
    column = lax.broadcasted_iota(jnp.int32, (128, LANES), 1)
    row_block, column_block = row >> 5, column >> 5
    first = (row_block > column_block) | ((row_block == column_block) & (row < column))
    for r in range(8):
        value = tile(r, r)
        mirrored = value.T
        put(scaled, r, r, jnp.where(row == column, F32(0.0), jnp.where(first, -value, mirrored)))
        put(plain, r, r, jnp.where(first, mirrored, value))
    for r in range(8):
        for step in (1, 2, 3, 4):
            c = (r + step) % 8
            if step == 4:
                if r >= 4:
                    continue
                one, other = tile(r, c), tile(c, r)
                is_eta = lax.rem(panel + r // 2, 4) < 2
                one_t, other_t = one.T, other.T
                put(scaled, r, c, jnp.where(is_eta, one_t, -other))
                put(scaled, c, r, jnp.where(is_eta, -one, other_t))
                put(plain, r, c, jnp.where(is_eta, other, one_t))
                put(plain, c, r, jnp.where(is_eta, other_t, one))
                continue
            p, q = (r, c) if SOURCE[r % 2][(c - r // 2 * 2) % 8] == 0 else (c, r)
            value = tile(p, q)
            put(scaled, q, p, -value)
            put(scaled, p, q, value.T)
            value = tile(q, p)
            put(plain, p, q, value)
            put(plain, q, p, value.T)
    for b in range(4):
        forward[b * 256 : (b + 1) * 256, :] = contract_last(scaled[b * 256 : (b + 1) * 256], plain[...])
    for b, ref in enumerate((own_out, plus_out, far_out, minus_out)):
        for l in range(2):
            for t, offset in enumerate(OFFSETS):
                r, c = 2 * b + l, (2 * b + l + offset) % 8
                value = forward[r * 128 : (r + 1) * 128, c * LANES : (c + 1) * LANES]
                other = forward[c * 128 : (c + 1) * 128, r * LANES : (r + 1) * LANES]
                ref[l, t] = (value + other.T).astype(BF16)


def part_kernel(own_ref, plus_ref, far_ref, minus_ref, out_ref):
    here = place()

    def pick(l, t, refs):
        value = refs[0][l, t]
        for k in range(1, 4):
            value = jnp.where(here == k, refs[k][l, t], value)
        return swap_blocks(value).astype(F32).reshape(16, 8, LANES)

    for l in range(2):
        low, high = [], []
        for t in range(5):
            pieces = interleave([pick(l, t, (own_ref, plus_ref, far_ref, minus_ref)), pick(l, t, (far_ref, minus_ref, own_ref, plus_ref))])
            low.append(pieces[0])
            high.append(pieces[1])
        out_ref[l * 32 : l * 32 + 16] = jnp.concatenate(low, axis=1).astype(BF16)
        out_ref[l * 32 + 16 : l * 32 + 32] = jnp.concatenate(high, axis=1).astype(BF16)


def recouple_back_kernel(table_ref, in_ref, out_ref):
    out_ref[...] = jnp.concatenate(recouple_rows(table_ref, in_ref, 5), axis=1).astype(BF16)


def back_tile(ref, l, t, ch):
    low = ref[l * 32 : l * 32 + 16].astype(F32)[:, t * 8 + ch * 4 : t * 8 + ch * 4 + 4]
    high = ref[l * 32 + 16 : l * 32 + 32].astype(F32)[:, t * 8 + ch * 4 : t * 8 + ch * 4 + 4]
    return jnp.concatenate([low, high], axis=1).reshape(128, LANES)


def back_mirror_kernel(in_ref, pp_ref, plus_ref, minus_ref, far_ref):
    for ch in range(2):
        for ref, held in ((plus_ref, PLUS), (minus_ref, MINUS), (far_ref, FAR)):
            for u, (l, t) in enumerate(held):
                ref[ch * len(held) + u] = (pp_ref[l, t, ch].T + back_tile(in_ref, l, t, ch)).astype(BF16)


def finish_kernel(in_ref, plus_ref, minus_ref, far_ref, pp_ref, out_ref):
    panel = lax.axis_index("panel")
    for ch in range(2):
        for l in range(2):

            def put(offset, value):
                out_ref[ch, l * 128 : (l + 1) * 128, pl.ds(tile_at(panel, l, offset), LANES)] = value.astype(BF16)

            for t, offset in enumerate(OFFSETS):
                put(offset, pp_ref[l, t, ch] + back_tile(in_ref, l, t, ch).T)
            put(2, minus_ref[ch * 2 + l])
            if l == 0:
                put(-1, plus_ref[ch * 2])
                put(-3, far_ref[ch])
            else:
                put(-1, pp_ref[0, 1, ch].T + back_tile(in_ref, 0, 1, ch))
                put(-3, plus_ref[ch * 2 + 1])


def contract_first(a, b):
    return lax.dot_general(a, b, (((0,), (0,)), ((), ())), preferred_element_type=F32)


def pair_kernel(eta_ref, gamma_ref, weight_ref, own_ref, plus_ref, far_ref, minus_ref, scaled, plain):
    panel = lax.axis_index("panel")
    for ch in range(2):
        for l in range(2):
            row = weight_ref[ch : ch + 1, pl.ds(tile_at(panel, l, 0), LANES)]
            weight = jnp.broadcast_to(row, (128, LANES)).T
            rows = slice(l * 128, (l + 1) * 128)
            for j in range(8):
                source = pl.ds(tile_at(panel, j, 0), LANES)
                columns = slice(j * LANES, (j + 1) * LANES)
                scaled[ch, rows, columns] = (eta_ref[ch, rows, source].astype(F32) * weight).astype(BF16)
                plain[ch, rows, columns] = gamma_ref[ch, rows, source]
        for owner, ref in enumerate((own_ref, plus_ref, far_ref, minus_ref)):
            columns = slice(owner * 256, (owner + 1) * 256)
            total = contract_first(scaled[ch, :, columns], plain[ch]) + contract_first(plain[ch, :, columns], scaled[ch])
            for l in range(2):
                for t, offset in enumerate(OFFSETS):
                    column = (2 * owner + l + offset) % 8 * LANES
                    ref[l, t, ch] = -total[l * 128 : (l + 1) * 128, column : column + LANES].astype(BF16)


def pair_sum_kernel(own_ref, plus_ref, far_ref, minus_ref, out_ref):
    for l in range(2):
        for t in range(5):
            for ch in range(2):
                parts = [ref[l, t, ch].astype(F32) for ref in (own_ref, plus_ref, far_ref, minus_ref)]
                out_ref[l, t, ch] = (parts[0] + parts[1]) + (parts[2] + parts[3])


def call(kernel, shapes, args, flops=0, scratch=(), name=None, dtype=BF16, space=None):
    single = not isinstance(shapes, list)
    outs = [shapes] if single else shapes
    types = dtype if isinstance(dtype, list) else [dtype] * len(outs)
    shaped = [jax.ShapeDtypeStruct(s, d) for s, d in zip(outs, types)]
    size = sum(a.size * a.dtype.itemsize for a in [*args, *shaped])
    return pl.pallas_call(
        kernel,
        out_shape=shaped[0] if single else shaped,
        in_specs=[pl.BlockSpec(memory_space=space or pltpu.VMEM)] * len(args),
        scratch_shapes=list(scratch),
        compiler_params=params(60 if space else 24),
        cost_estimate=cost(flops, size),
        name=name,
    )(*args)


def exchange(operand, axis):
    return lax.all_to_all(operand, axis, split_axis=0, concat_axis=0, tiled=True)


def step(value, by):
    return lax.ppermute(value, "panel", [(i, (i + by) % 4) for i in range(4)])


def mirror(plus, minus, far):
    return step(plus, 1), step(minus, 3), step(far, 2)


def route(value, by, places):
    pairs = []
    for chan in range(64):
        for here in places:
            panel = (here + chan % 2) % 4
            pairs.append((chan * 4 + panel, chan * 4 + (panel + by) % 4))
    return lax.ppermute(value, ("chan", "panel"), pairs)


def to_owner(plus, minus, far):
    return route(plus, 1, (1, 3)), route(minus, 3, (1, 3)), route(far, 2, (0, 2))


def from_owner(plus, far, minus):
    return route(plus, 1, (0, 2)), route(far, 2, (0, 2)), route(minus, 3, (0, 2))


def shards(eta, gamma, pp_weight, cc_weight, live_pairs, forward_table, back_table):
    positions = lax.broadcasted_iota(jnp.int32, pp_weight.shape, 1)
    weight_pp = jnp.where(positions < live_pairs[:, None], pp_weight, F32(0.0))
    packed = call(
        pack_kernel,
        (64, 64, LANES),
        (eta, gamma),
        scratch=[pltpu.VMEM((2, 2, 256, 1024), BF16), pltpu.SemaphoreType.DMA((2, 2, 2))],
        name="pack",
        space=pltpu.HBM,
    )
    forward_wide, back_wide = call(spread_kernel, [(512, 512)] * 2, (forward_table, back_table), flops=300_000_000, name="spread")
    packed = exchange(packed, "chan")
    pp_own, *pp = call(
        pair_kernel,
        [(2, 5, 2, 128, LANES)] * 4,
        (eta, gamma, weight_pp),
        flops=2_200_000_000,
        scratch=[pltpu.VMEM((2, 256, 1024), BF16)] * 2,
        name="pair",
    )
    pp_plus, pp_minus = step(pp[0], 1), step(pp[2], 3)
    packed, pp_own, pp_far, pp_plus, pp_minus = lax.optimization_barrier((packed, pp_own, pp[1], pp_plus, pp_minus))
    mixed = call(recouple_kernel, (64, 64, LANES), (forward_wide, packed), flops=700_000_000, name="recouple")
    mixed = exchange(mixed, "chan")
    pp_far = step(pp_far, 2)
    pp_part = call(pair_sum_kernel, (2, 5, 2, 128, LANES), (pp_own, pp_plus, pp_far, pp_minus), name="pair_sum", dtype=F32)
    mixed, pp_part = lax.optimization_barrier((mixed, pp_part))
    sends = call(send_kernel, [(64, 32, LANES)] * 3, (mixed,), name="send")
    received = to_owner(*sends)
    own, *outs = call(
        product_kernel,
        [(2, 5, 128, LANES)] * 4,
        (mixed, *received, cc_weight),
        flops=2_200_000_000,
        scratch=[pltpu.VMEM((1024, 1024), BF16)] * 2 + [pltpu.VMEM((1024, 1024), F32)],
        name="product",
    )
    outs = from_owner(*outs)
    part = call(part_kernel, (64, 40, LANES), (own, *outs), name="part")
    part = exchange(part, "chan")
    part = call(recouple_back_kernel, (64, 40, LANES), (back_wide, part), flops=400_000_000, name="recouple_back")
    part = exchange(part, "chan")
    back_sends = call(back_mirror_kernel, [(4, 128, LANES), (4, 128, LANES), (2, 128, LANES)], (part, pp_part), name="back_mirror")
    back_received = mirror(*back_sends)
    return call(finish_kernel, (2, 256, 1024), (part, *back_received, pp_part), name="finish")


def solution(mesh):
    in_specs = (
        P("chan", "panel", None),
        P("chan", "panel", None),
        P("chan", None),
        P("chan", None),
        P("chan"),
        P(),
        P(),
    )
    out_specs = P("chan", "panel", None)
    return jax.shard_map(shards, mesh=mesh, in_specs=in_specs, out_specs=out_specs, check_vma=False)
```

```python
import jax
import jax.numpy as jnp
from jax import lax
from jax.experimental import pallas as pl
from jax.experimental.pallas import tpu as pltpu
from jax.sharding import PartitionSpec as P

BF16 = jnp.bfloat16
F32 = jnp.float32
OFFSETS = (0, 1, -2, 3, 4)
LANES = 128


def params(mib=24):
    return pltpu.CompilerParams(vmem_limit_bytes=mib * 1024 * 1024)


def cost(flops, size):
    return pl.CostEstimate(flops=flops, bytes_accessed=size, transcendentals=0)


def tile_at(panel, l, offset):
    return pl.multiple_of(lax.rem(2 * panel + l + offset + 8, 8) * LANES, LANES)


def swap_blocks(x):
    lane = lax.broadcasted_iota(jnp.int32, (64, LANES), 1)
    top, bottom = x[:64], x[64:]
    low = lane < 64
    upper = jnp.where(low, top, pltpu.roll(bottom, 64, 1))
    lower = jnp.where(low, pltpu.roll(top, 64, 1), bottom)
    even = (lane[:32] & 32) == 0
    parts = []
    for half in (upper, lower):
        first, second = half[:32], half[32:]
        parts.append(jnp.where(even, first, pltpu.roll(second, 32, 1)))
        parts.append(jnp.where(even, pltpu.roll(first, 96, 1), second))
    return jnp.concatenate(parts, axis=0)


def masks():
    row = lax.broadcasted_iota(jnp.int32, (128, LANES), 0)
    column = lax.broadcasted_iota(jnp.int32, (128, LANES), 1)
    row_block, column_block = row >> 5, column >> 5
    return (row_block > column_block) | ((row_block == column_block) & (row < column)), row == column


def contract_last(a, b):
    return lax.dot_general(a, b, (((1,), (1,)), ((), ())), preferred_element_type=F32)


def interleave(both):
    return [jnp.concatenate([both[0][:, r : r + 4], both[1][:, r : r + 4]], axis=1) for r in (0, 4)]


SOURCE = ((2, 0, 0, 0, 3, 0, 1, 1), (1, 2, 0, 0, 1, 3, 1, 1))


def pack_kernel(eta_ref, gamma_ref, out_ref, held, ready, sems, out_sems):
    panel = lax.axis_index("panel")
    either = jnp.where(panel < 2, 0, 1)
    row = lax.broadcasted_iota(jnp.int32, (128, LANES), 0)
    column = lax.broadcasted_iota(jnp.int32, (128, LANES), 1)
    copies = {}
    for l in range(2):
        for ch in range(2):
            for arr, ref in enumerate((eta_ref, gamma_ref)):
                rows = slice(l * 128, (l + 1) * 128)
                copy = pltpu.make_async_copy(ref.at[ch, rows], held.at[arr, ch, rows], sems.at[l, ch, arr])
                copy.start()
                copies[l, ch, arr] = copy

    def tile(ch, l, j):
        def read(arr):
            return held[arr, ch, l * 128 : (l + 1) * 128, pl.ds(tile_at(panel, j, 0), LANES)]

        kind = SOURCE[l][j]
        value = jnp.where(row < column, read(0), read(1)) if kind == 2 else read(either if kind == 3 else kind)
        return swap_blocks(value).astype(F32).reshape(16, 8, LANES)

    for l in range(2):
        for ch in range(2):
            for arr in range(2):
                copies[l, ch, arr].wait()
        for part in range(2):
            pieces = []
            for j in range(part * 4, part * 4 + 4):
                pieces += interleave([tile(ch, l, j) for ch in range(2)])
            rows = slice(part * 32 + l * 16, part * 32 + l * 16 + 16)
            ready[rows] = jnp.concatenate(pieces, axis=1).astype(BF16)
            copies[l, part] = pltpu.make_async_copy(ready.at[rows], out_ref.at[rows], out_sems.at[l, part])
            copies[l, part].start()
    for l in range(2):
        for part in range(2):
            copies[l, part].wait()


def spread_kernel(forward_ref, back_ref, forward_out, back_out, edge_out):
    for ref, out, shift in ((forward_ref, forward_out, 2), (back_ref, back_out, 2), (back_ref, edge_out, 1)):
        size = 128 << shift
        row = lax.broadcasted_iota(jnp.int32, (size, 128), 0) >> shift
        column = lax.broadcasted_iota(jnp.int32, (size, 128), 1)
        copies = jnp.where(row == column, F32(1.0), F32(0.0)).astype(BF16)
        tall = jnp.dot(copies, ref[...], preferred_element_type=F32).astype(BF16)
        mask = (1 << shift) - 1
        for start in range(0, size, 256):
            wide = contract_last(tall[start : start + 256], copies)
            row = lax.broadcasted_iota(jnp.int32, wide.shape, 0) & mask
            column = lax.broadcasted_iota(jnp.int32, wide.shape, 1) & mask
            out[start : start + 256, :] = jnp.where(row == column, wide, F32(0.0)).astype(BF16)


def recouple_rows(table_ref, in_ref, count):
    value = in_ref[...].astype(F32)
    rhs = jnp.concatenate([value[:, q * 8 : q * 8 + 8].reshape(512, LANES) for q in range(count)], axis=1).astype(BF16)
    mixed = jnp.dot(table_ref[...], rhs, preferred_element_type=F32)
    return [mixed[:, q * LANES : (q + 1) * LANES].reshape(64, 8, LANES) for q in range(count)]


def recouple_kernel(table_ref, in_ref, out_ref):
    pieces = recouple_rows(table_ref, in_ref, 8)
    for ch in range(2):
        rows = [piece[:, ch * 4 : ch * 4 + 4] for piece in pieces]
        out_ref[:, ch * 32 : ch * 32 + 32] = jnp.concatenate(rows, axis=1).astype(BF16)


PLUS = ((1, 1), (0, 3))
MINUS = ((0, 2), (1, 2))
FAR = ((1, 3),)


def place():
    return lax.rem(lax.axis_index("panel") + 4 - lax.rem(lax.axis_index("chan"), 2), 4)


def send_kernel(in_ref, plus_ref, minus_ref, far_ref):
    here = place()

    def rows(ch):
        return in_ref[:, pl.ds(pl.multiple_of(ch * 32, 32), 32), :]

    plus_ref[...] = rows(jnp.where(here == 1, 1, 0))
    minus_ref[...] = rows(jnp.where(here == 1, 0, 1))
    far_ref[...] = rows(jnp.where(here == 0, 1, 0))


def tile_of(ref, l, j, first=0):
    start = j // 4 * 32 + l * 16
    return ref[start : start + 16, pl.ds(first, 32), :].astype(F32)[:, j % 4 * 8 : j % 4 * 8 + 8].reshape(128, LANES)


def product_kernel(in_ref, plus_ref, minus_ref, far_ref, weight_ref, own_out, plus_out, far_out, minus_out, scaled, plain, forward):
    panel = lax.axis_index("panel")
    own = jnp.where(place() == 2, 1, 0)

    def tile(r, c):
        b, l = divmod(r, 2)
        j = (c - 2 * b) % 8
        if b == 0:
            return tile_of(in_ref, l, j, pl.multiple_of(own * 32, 32))
        return tile_of((minus_ref, far_ref, plus_ref)[b - 1], l, j)

    lanes = []
    for j in range(8):
        columns = pl.ds(tile_at(panel, j, 0), LANES)
        lanes.append(jnp.where(own == 0, weight_ref[0:1, columns], weight_ref[1:2, columns]))

    def put(ref, r, c, value):
        if ref is scaled:
            value = value * lanes[c]
        ref[r * 128 : (r + 1) * 128, c * LANES : (c + 1) * LANES] = value.astype(BF16)

    first, diagonal = masks()
    for r in range(8):
        value = tile(r, r)
        mirrored = value.T
        put(scaled, r, r, jnp.where(diagonal, F32(0.0), jnp.where(first, -value, mirrored)))
        put(plain, r, r, jnp.where(first, mirrored, value))
    for r in range(8):
        for step in (1, 2, 3, 4):
            c = (r + step) % 8
            if step == 4:
                if r >= 4:
                    continue
                one, other = tile(r, c), tile(c, r)
                is_eta = lax.rem(panel + r // 2, 4) < 2
                one_t, other_t = one.T, other.T
                put(scaled, r, c, jnp.where(is_eta, one_t, -other))
                put(scaled, c, r, jnp.where(is_eta, -one, other_t))
                put(plain, r, c, jnp.where(is_eta, other, one_t))
                put(plain, c, r, jnp.where(is_eta, other_t, one))
                continue
            p, q = (r, c) if SOURCE[r % 2][(c - r // 2 * 2) % 8] == 0 else (c, r)
            value = tile(p, q)
            put(scaled, q, p, -value)
            put(scaled, p, q, value.T)
            value = tile(q, p)
            put(plain, p, q, value)
            put(plain, q, p, value.T)
    for b in range(4):
        forward[b * 256 : (b + 1) * 256, :] = contract_last(scaled[b * 256 : (b + 1) * 256], plain[...])

    def product(r, offset):
        c = (r + offset) % 8
        value = forward[r * 128 : (r + 1) * 128, c * LANES : (c + 1) * LANES]
        return value + forward[c * 128 : (c + 1) * 128, r * LANES : (r + 1) * LANES].T

    above = lax.broadcasted_iota(jnp.int32, (128, LANES), 0) < lax.broadcasted_iota(jnp.int32, (128, LANES), 1)
    for b, ref in enumerate((own_out, plus_out, far_out, minus_out)):
        edges = []
        for l in range(2):
            r = 2 * b + l
            across = product(r, 4)
            edges.append(jnp.sum(jnp.where(diagonal, across, F32(0.0)), axis=0, keepdims=True))
            tiles = [jnp.where(above, across, product(r, 0))] + [product(r, offset) for offset in OFFSETS[1:4]]
            for t, value in enumerate(tiles):
                start = (l * 4 + t) * 128
                ref[start : start + 128] = value.astype(BF16)
        ref[1024:1040] = jnp.concatenate(edges + [jnp.zeros((14, LANES), F32)], axis=0).astype(BF16)


def part_kernel(own_ref, plus_ref, far_ref, minus_ref, out_ref):
    here = place()
    orders = ((own_ref, plus_ref, far_ref, minus_ref), (far_ref, minus_ref, own_ref, plus_ref))

    def pick(ch, start, size):
        value = orders[ch][0][start : start + size]
        for k in range(1, 4):
            value = jnp.where(here == k, orders[ch][k][start : start + size], value)
        return value

    edges = [pick(ch, 1024, 16).astype(F32)[:2] for ch in range(2)]
    edges = jnp.concatenate(edges + [jnp.zeros((4, LANES), F32)], axis=0)
    edges = jnp.broadcast_to(edges[None], (16, 8, LANES))
    for l in range(2):
        low, high = [], []
        for t in range(4):
            both = [swap_blocks(pick(ch, (l * 4 + t) * 128, 128)).astype(F32).reshape(16, 8, LANES) for ch in range(2)]
            pieces = interleave(both)
            low.append(pieces[0])
            high.append(pieces[1])
        out_ref[l * 32 : l * 32 + 16] = jnp.concatenate(low + [edges], axis=1).astype(BF16)
        out_ref[l * 32 + 16 : l * 32 + 32] = jnp.concatenate(high + [edges], axis=1).astype(BF16)


def recouple_back_kernel(table_ref, edge_table_ref, in_ref, out_ref, edge_ref, mixed):
    out_ref[...] = jnp.concatenate(recouple_rows(table_ref, in_ref, 4), axis=1).astype(BF16)
    edges = in_ref[:, 32:40, :].astype(F32).reshape(32, 2, 8, LANES)
    edges = jnp.concatenate([edges[:, 0, :4], edges[:, 1, :4]], axis=1).reshape(256, LANES).astype(BF16)
    mixed[...] = jnp.dot(edge_table_ref[...], edges, preferred_element_type=F32).astype(BF16).astype(F32)
    edge_ref[...] = mixed[pl.ds(pl.multiple_of(lax.axis_index("chan") * 4, 4), 4), :]


def back_tile(ref, l, t, ch):
    low = ref[l * 32 : l * 32 + 16].astype(F32)[:, t * 8 + ch * 4 : t * 8 + ch * 4 + 4]
    high = ref[l * 32 + 16 : l * 32 + 32].astype(F32)[:, t * 8 + ch * 4 : t * 8 + ch * 4 + 4]
    return jnp.concatenate([low, high], axis=1).reshape(128, LANES)


def back_mirror_kernel(in_ref, pp_ref, plus_ref, minus_ref, far_ref):
    for ch in range(2):
        for ref, held, size in ((plus_ref, PLUS, 2), (minus_ref, MINUS, 2), (far_ref, FAR, 3)):
            for u, (l, t) in enumerate(held):
                ref[ch * size + u] = (pp_ref[l, t, ch].T + back_tile(in_ref, l, t, ch)).astype(BF16)
        for l in range(2):
            far_ref[ch * 3 + 1 + l] = back_tile(in_ref, l, 0, ch).astype(BF16)


def finish_kernel(in_ref, plus_ref, minus_ref, far_ref, pp_ref, edge_ref, out_ref):
    panel = lax.axis_index("panel")
    first, diagonal = masks()
    for ch in range(2):
        for l in range(2):

            def put(offset, value):
                out_ref[ch, l * 128 : (l + 1) * 128, pl.ds(tile_at(panel, l, offset), LANES)] = value.astype(BF16)

            value = back_tile(in_ref, l, 0, ch)
            mirrored = value.T
            put(0, pp_ref[l, 0, ch] + jnp.where(first, mirrored, value))
            edge = edge_ref[ch * 2 + l : ch * 2 + l + 1]
            across = jnp.where(first, far_ref[ch * 3 + 1 + l].astype(F32), jnp.where(diagonal, edge, mirrored))
            put(4, pp_ref[l, 4, ch] + across)
            for t in (1, 2, 3):
                put(OFFSETS[t], pp_ref[l, t, ch] + back_tile(in_ref, l, t, ch).T)
            put(2, minus_ref[ch * 2 + l])
            if l == 0:
                put(-1, plus_ref[ch * 2])
                put(-3, far_ref[ch * 3])
            else:
                put(-1, pp_ref[0, 1, ch].T + back_tile(in_ref, 0, 1, ch))
                put(-3, plus_ref[ch * 2 + 1])


def contract_first(a, b):
    return lax.dot_general(a, b, (((0,), (0,)), ((), ())), preferred_element_type=F32)


def pair_kernel(eta_ref, gamma_ref, weight_ref, own_ref, plus_ref, far_ref, minus_ref, scaled, plain):
    panel = lax.axis_index("panel")
    for ch in range(2):
        for l in range(2):
            row = weight_ref[ch : ch + 1, pl.ds(tile_at(panel, l, 0), LANES)]
            weight = jnp.broadcast_to(row, (128, LANES)).T
            rows = slice(l * 128, (l + 1) * 128)
            for j in range(8):
                source = pl.ds(tile_at(panel, j, 0), LANES)
                columns = slice(j * LANES, (j + 1) * LANES)
                scaled[ch, rows, columns] = (eta_ref[ch, rows, source].astype(F32) * weight).astype(BF16)
                plain[ch, rows, columns] = gamma_ref[ch, rows, source]
        for owner, ref in enumerate((own_ref, plus_ref, far_ref, minus_ref)):
            columns = slice(owner * 256, (owner + 1) * 256)
            total = contract_first(scaled[ch, :, columns], plain[ch]) + contract_first(plain[ch, :, columns], scaled[ch])
            for l in range(2):
                for t, offset in enumerate(OFFSETS):
                    column = (2 * owner + l + offset) % 8 * LANES
                    ref[l, t, ch] = -total[l * 128 : (l + 1) * 128, column : column + LANES].astype(BF16)


def pair_sum_kernel(own_ref, plus_ref, far_ref, minus_ref, out_ref):
    for l in range(2):
        for t in range(5):
            for ch in range(2):
                parts = [ref[l, t, ch].astype(F32) for ref in (own_ref, plus_ref, far_ref, minus_ref)]
                out_ref[l, t, ch] = (parts[0] + parts[1]) + (parts[2] + parts[3])


def call(kernel, shapes, args, flops=0, scratch=(), name=None, dtype=BF16, space=None):
    single = not isinstance(shapes, list)
    outs = [shapes] if single else shapes
    types = dtype if isinstance(dtype, list) else [dtype] * len(outs)
    shaped = [jax.ShapeDtypeStruct(s, d) for s, d in zip(outs, types)]
    size = sum(a.size * a.dtype.itemsize for a in [*args, *shaped])
    return pl.pallas_call(
        kernel,
        out_shape=shaped[0] if single else shaped,
        in_specs=[pl.BlockSpec(memory_space=space or pltpu.VMEM)] * len(args),
        out_specs=jax.tree.map(lambda _: pl.BlockSpec(memory_space=space or pltpu.VMEM), shaped[0] if single else shaped),
        scratch_shapes=list(scratch),
        compiler_params=params(60 if space else 24),
        cost_estimate=cost(flops, size),
        name=name,
    )(*args)


def exchange(operand, axis):
    return lax.all_to_all(operand, axis, split_axis=0, concat_axis=0, tiled=True)


def step(value, by):
    return lax.ppermute(value, "panel", [(i, (i + by) % 4) for i in range(4)])


def mirror(plus, minus, far):
    return step(plus, 1), step(minus, 3), step(far, 2)


def route(value, by, places):
    pairs = []
    for chan in range(64):
        for here in places:
            panel = (here + chan % 2) % 4
            pairs.append((chan * 4 + panel, chan * 4 + (panel + by) % 4))
    return lax.ppermute(value, ("chan", "panel"), pairs)


def to_owner(plus, minus, far):
    return route(plus, 1, (1, 3)), route(minus, 3, (1, 3)), route(far, 2, (0, 2))


def from_owner(plus, far, minus):
    return route(plus, 1, (0, 2)), route(far, 2, (0, 2)), route(minus, 3, (0, 2))


def shards(eta, gamma, pp_weight, cc_weight, live_pairs, forward_table, back_table):
    positions = lax.broadcasted_iota(jnp.int32, pp_weight.shape, 1)
    weight_pp = jnp.where(positions < live_pairs[:, None], pp_weight, F32(0.0))
    packed = call(
        pack_kernel,
        (64, 64, LANES),
        (eta, gamma),
        scratch=[
            pltpu.VMEM((2, 2, 256, 1024), BF16),
            pltpu.VMEM((64, 64, LANES), BF16),
            pltpu.SemaphoreType.DMA((2, 2, 2)),
            pltpu.SemaphoreType.DMA((2, 2)),
        ],
        name="pack",
        space=pltpu.HBM,
    )
    forward_wide, back_wide, edge_wide = call(spread_kernel, [(512, 512), (512, 512), (256, 256)], (forward_table, back_table), flops=300_000_000, name="spread")
    packed = exchange(packed, "chan")
    pp_own, *pp = call(
        pair_kernel,
        [(2, 5, 2, 128, LANES)] * 4,
        (eta, gamma, weight_pp),
        flops=2_200_000_000,
        scratch=[pltpu.VMEM((2, 256, 1024), BF16)] * 2,
        name="pair",
    )
    pp_plus, pp_minus = step(pp[0], 1), step(pp[2], 3)
    packed, pp_own, pp_far, pp_plus, pp_minus = lax.optimization_barrier((packed, pp_own, pp[1], pp_plus, pp_minus))
    mixed = call(recouple_kernel, (64, 64, LANES), (forward_wide, packed), flops=700_000_000, name="recouple")
    mixed = exchange(mixed, "chan")
    pp_far = step(pp_far, 2)
    pp_part = call(pair_sum_kernel, (2, 5, 2, 128, LANES), (pp_own, pp_plus, pp_far, pp_minus), name="pair_sum", dtype=F32)
    mixed, pp_part = lax.optimization_barrier((mixed, pp_part))
    sends = call(send_kernel, [(64, 32, LANES)] * 3, (mixed,), name="send")
    received = to_owner(*sends)
    own, *outs = call(
        product_kernel,
        [(1040, LANES)] * 4,
        (mixed, *received, cc_weight),
        flops=2_200_000_000,
        scratch=[pltpu.VMEM((1024, 1024), BF16)] * 2 + [pltpu.VMEM((1024, 1024), F32)],
        name="product",
    )
    outs = from_owner(*outs)
    part = call(part_kernel, (64, 40, LANES), (own, *outs), name="part")
    part = exchange(part, "chan")
    part, edge = call(
        recouple_back_kernel,
        [(64, 32, LANES), (4, LANES)],
        (back_wide, edge_wide, part),
        flops=400_000_000,
        scratch=[pltpu.VMEM((256, LANES), F32)],
        name="recouple_back",
        dtype=[BF16, F32],
    )
    part = exchange(part, "chan")
    back_sends = call(back_mirror_kernel, [(4, 128, LANES), (4, 128, LANES), (6, 128, LANES)], (part, pp_part), name="back_mirror")
    back_received = mirror(*back_sends)
    return call(finish_kernel, (2, 256, 1024), (part, *back_received, pp_part, edge), name="finish")


def solution(mesh):
    in_specs = (
        P("chan", "panel", None),
        P("chan", "panel", None),
        P("chan", None),
        P("chan", None),
        P("chan"),
        P(),
        P(),
    )
    out_specs = P("chan", "panel", None)
    return jax.shard_map(shards, mesh=mesh, in_specs=in_specs, out_specs=out_specs, check_vma=False)
```

```python
import jax
import jax.numpy as jnp
from jax import lax
from jax.experimental import pallas as pl
from jax.experimental.pallas import tpu as pltpu
from jax.sharding import PartitionSpec as P

BF16 = jnp.bfloat16
F32 = jnp.float32
OFFSETS = (0, 1, -2, 3, 4)
LANES = 128


def params(mib=24):
    return pltpu.CompilerParams(vmem_limit_bytes=mib * 1024 * 1024)


def cost(flops, size):
    return pl.CostEstimate(flops=flops, bytes_accessed=size, transcendentals=0)


def tile_at(panel, l, offset):
    return pl.multiple_of(lax.rem(2 * panel + l + offset + 8, 8) * LANES, LANES)


def swap_blocks(x):
    lane = lax.broadcasted_iota(jnp.int32, (64, LANES), 1)
    top, bottom = x[:64], x[64:]
    low = lane < 64
    upper = jnp.where(low, top, pltpu.roll(bottom, 64, 1))
    lower = jnp.where(low, pltpu.roll(top, 64, 1), bottom)
    even = (lane[:32] & 32) == 0
    parts = []
    for half in (upper, lower):
        first, second = half[:32], half[32:]
        parts.append(jnp.where(even, first, pltpu.roll(second, 32, 1)))
        parts.append(jnp.where(even, pltpu.roll(first, 96, 1), second))
    return jnp.concatenate(parts, axis=0)


def masks():
    row = lax.broadcasted_iota(jnp.int32, (128, LANES), 0)
    column = lax.broadcasted_iota(jnp.int32, (128, LANES), 1)
    row_block, column_block = row >> 5, column >> 5
    return (row_block > column_block) | ((row_block == column_block) & (row < column)), row == column


def contract_last(a, b):
    return lax.dot_general(a, b, (((1,), (1,)), ((), ())), preferred_element_type=F32)


def interleave(both):
    return [jnp.concatenate([both[0][:, r : r + 4], both[1][:, r : r + 4]], axis=1) for r in (0, 4)]


SOURCE = ((2, 0, 0, 0, 3, 0, 1, 1), (1, 2, 0, 0, 1, 3, 1, 1))


def pack_kernel(eta_ref, gamma_ref, out_ref, held, ready, sems, out_sems):
    panel = lax.axis_index("panel")
    either = jnp.where(panel < 2, 0, 1)
    row = lax.broadcasted_iota(jnp.int32, (128, LANES), 0)
    column = lax.broadcasted_iota(jnp.int32, (128, LANES), 1)
    copies = {}
    for l in range(2):
        for ch in range(2):
            for arr, ref in enumerate((eta_ref, gamma_ref)):
                rows = slice(l * 128, (l + 1) * 128)
                copy = pltpu.make_async_copy(ref.at[ch, rows], held.at[arr, ch, rows], sems.at[l, ch, arr])
                copy.start()
                copies[l, ch, arr] = copy

    def tile(ch, l, j):
        def read(arr):
            return held[arr, ch, l * 128 : (l + 1) * 128, pl.ds(tile_at(panel, j, 0), LANES)]

        kind = SOURCE[l][j]
        value = jnp.where(row < column, read(0), read(1)) if kind == 2 else read(either if kind == 3 else kind)
        return swap_blocks(value).astype(F32).reshape(16, 8, LANES)

    for l in range(2):
        for ch in range(2):
            for arr in range(2):
                copies[l, ch, arr].wait()
        for part in range(2):
            pieces = []
            for j in range(part * 4, part * 4 + 4):
                pieces += interleave([tile(ch, l, j) for ch in range(2)])
            rows = slice(part * 32 + l * 16, part * 32 + l * 16 + 16)
            ready[rows] = jnp.concatenate(pieces, axis=1).astype(BF16)
            copies[l, part] = pltpu.make_async_copy(ready.at[rows], out_ref.at[rows], out_sems.at[l, part])
            copies[l, part].start()
    for l in range(2):
        for part in range(2):
            copies[l, part].wait()


def spread_kernel(forward_ref, back_ref, forward_out, back_out, edge_out):
    for ref, out, shift in ((forward_ref, forward_out, 2), (back_ref, back_out, 2), (back_ref, edge_out, 1)):
        size = 128 << shift
        row = lax.broadcasted_iota(jnp.int32, (size, 128), 0) >> shift
        column = lax.broadcasted_iota(jnp.int32, (size, 128), 1)
        copies = jnp.where(row == column, F32(1.0), F32(0.0)).astype(BF16)
        tall = jnp.dot(copies, ref[...], preferred_element_type=F32).astype(BF16)
        mask = (1 << shift) - 1
        for start in range(0, size, 256):
            wide = contract_last(tall[start : start + 256], copies)
            row = lax.broadcasted_iota(jnp.int32, wide.shape, 0) & mask
            column = lax.broadcasted_iota(jnp.int32, wide.shape, 1) & mask
            out[start : start + 256, :] = jnp.where(row == column, wide, F32(0.0)).astype(BF16)


def recouple_rows(table_ref, in_ref, count):
    value = in_ref[...].astype(F32)
    rhs = jnp.concatenate([value[:, q * 8 : q * 8 + 8].reshape(512, LANES) for q in range(count)], axis=1).astype(BF16)
    mixed = jnp.dot(table_ref[...], rhs, preferred_element_type=F32)
    return [mixed[:, q * LANES : (q + 1) * LANES].reshape(64, 8, LANES) for q in range(count)]


def recouple_kernel(table_ref, in_ref, out_ref):
    pieces = recouple_rows(table_ref, in_ref, 8)
    for ch in range(2):
        rows = [piece[:, ch * 4 : ch * 4 + 4] for piece in pieces]
        out_ref[:, ch * 32 : ch * 32 + 32] = jnp.concatenate(rows, axis=1).astype(BF16)


PLUS = ((1, 1), (0, 3))
MINUS = ((0, 2), (1, 2))
FAR = ((1, 3),)


def place():
    return lax.rem(lax.axis_index("panel") + 4 - lax.rem(lax.axis_index("chan"), 2), 4)


def channel_rows(ref, ch):
    return ref[:, pl.ds(pl.multiple_of(ch * 32, 32), 32), :]


def send_far_kernel(in_ref, far_ref):
    far_ref[...] = channel_rows(in_ref, jnp.where(place() == 0, 1, 0))


def send_near_kernel(in_ref, plus_ref, minus_ref):
    here = place()
    plus_ref[...] = channel_rows(in_ref, jnp.where(here == 1, 1, 0))
    minus_ref[...] = channel_rows(in_ref, jnp.where(here == 1, 0, 1))


def tile_of(ref, l, j, first=0):
    start = j // 4 * 32 + l * 16
    return ref[start : start + 16, pl.ds(first, 32), :].astype(F32)[:, j % 4 * 8 : j % 4 * 8 + 8].reshape(128, LANES)


def product_kernel(in_ref, plus_ref, minus_ref, far_ref, weight_ref, own_out, plus_out, far_out, minus_out, scaled, plain, forward):
    panel = lax.axis_index("panel")
    own = jnp.where(place() == 2, 1, 0)

    def tile(r, c):
        b, l = divmod(r, 2)
        j = (c - 2 * b) % 8
        if b == 0:
            return tile_of(in_ref, l, j, pl.multiple_of(own * 32, 32))
        return tile_of((minus_ref, far_ref, plus_ref)[b - 1], l, j)

    lanes = []
    for j in range(8):
        columns = pl.ds(tile_at(panel, j, 0), LANES)
        lanes.append(jnp.where(own == 0, weight_ref[0:1, columns], weight_ref[1:2, columns]))

    def put(ref, r, c, value):
        if ref is scaled:
            value = value * lanes[c]
        ref[r * 128 : (r + 1) * 128, c * LANES : (c + 1) * LANES] = value.astype(BF16)

    first, diagonal = masks()
    for r in range(8):
        value = tile(r, r)
        mirrored = value.T
        put(scaled, r, r, jnp.where(diagonal, F32(0.0), jnp.where(first, -value, mirrored)))
        put(plain, r, r, jnp.where(first, mirrored, value))
    for r in range(8):
        for step in (1, 2, 3, 4):
            c = (r + step) % 8
            if step == 4:
                if r >= 4:
                    continue
                one, other = tile(r, c), tile(c, r)
                is_eta = lax.rem(panel + r // 2, 4) < 2
                one_t, other_t = one.T, other.T
                put(scaled, r, c, jnp.where(is_eta, one_t, -other))
                put(scaled, c, r, jnp.where(is_eta, -one, other_t))
                put(plain, r, c, jnp.where(is_eta, other, one_t))
                put(plain, c, r, jnp.where(is_eta, other_t, one))
                continue
            p, q = (r, c) if SOURCE[r % 2][(c - r // 2 * 2) % 8] == 0 else (c, r)
            value = tile(p, q)
            put(scaled, q, p, -value)
            put(scaled, p, q, value.T)
            value = tile(q, p)
            put(plain, p, q, value)
            put(plain, q, p, value.T)
    for b in range(4):
        forward[b * 256 : (b + 1) * 256, :] = contract_last(scaled[b * 256 : (b + 1) * 256], plain[...])

    def product(r, offset):
        c = (r + offset) % 8
        value = forward[r * 128 : (r + 1) * 128, c * LANES : (c + 1) * LANES]
        return value + forward[c * 128 : (c + 1) * 128, r * LANES : (r + 1) * LANES].T

    above = lax.broadcasted_iota(jnp.int32, (128, LANES), 0) < lax.broadcasted_iota(jnp.int32, (128, LANES), 1)
    for b, ref in enumerate((own_out, plus_out, far_out, minus_out)):
        edges = []
        for l in range(2):
            r = 2 * b + l
            across = product(r, 4)
            edges.append(jnp.sum(jnp.where(diagonal, across, F32(0.0)), axis=0, keepdims=True))
            tiles = [jnp.where(above, across, product(r, 0))] + [product(r, offset) for offset in OFFSETS[1:4]]
            for t, value in enumerate(tiles):
                start = (l * 4 + t) * 128
                ref[start : start + 128] = value.astype(BF16)
        if b == 2:
            ref[1040:1056] = jnp.zeros((16, LANES), BF16)
        ref[1024:1040] = jnp.concatenate(edges + [jnp.zeros((14, LANES), F32)], axis=0).astype(BF16)


def part_kernel(own_ref, plus_ref, far_ref, minus_ref, out_ref):
    here = place()
    orders = ((own_ref, plus_ref, far_ref, minus_ref), (far_ref, minus_ref, own_ref, plus_ref))

    def pick(ch, start, size):
        value = orders[ch][0][start : start + size]
        for k in range(1, 4):
            value = jnp.where(here == k, orders[ch][k][start : start + size], value)
        return value

    edges = [pick(ch, 1024, 16).astype(F32)[:2] for ch in range(2)]
    edges = jnp.concatenate(edges + [jnp.zeros((4, LANES), F32)], axis=0)
    edges = jnp.broadcast_to(edges[None], (16, 8, LANES))
    for l in range(2):
        low, high = [], []
        for t in range(4):
            both = [swap_blocks(pick(ch, (l * 4 + t) * 128, 128)).astype(F32).reshape(16, 8, LANES) for ch in range(2)]
            pieces = interleave(both)
            low.append(pieces[0])
            high.append(pieces[1])
        out_ref[l * 32 : l * 32 + 16] = jnp.concatenate(low + [edges], axis=1).astype(BF16)
        out_ref[l * 32 + 16 : l * 32 + 32] = jnp.concatenate(high + [edges], axis=1).astype(BF16)


def recouple_back_kernel(table_ref, edge_table_ref, in_ref, out_ref, edge_ref, mixed):
    out_ref[...] = jnp.concatenate(recouple_rows(table_ref, in_ref, 4), axis=1).astype(BF16)
    edges = in_ref[:, 32:40, :].astype(F32).reshape(32, 2, 8, LANES)
    edges = jnp.concatenate([edges[:, 0, :4], edges[:, 1, :4]], axis=1).reshape(256, LANES).astype(BF16)
    mixed[...] = jnp.dot(edge_table_ref[...], edges, preferred_element_type=F32).astype(BF16).astype(F32)
    edge_ref[...] = mixed[pl.ds(pl.multiple_of(lax.axis_index("chan") * 4, 4), 4), :]


def back_tile(ref, l, t, ch):
    low = ref[l * 32 : l * 32 + 16].astype(F32)[:, t * 8 + ch * 4 : t * 8 + ch * 4 + 4]
    high = ref[l * 32 + 16 : l * 32 + 32].astype(F32)[:, t * 8 + ch * 4 : t * 8 + ch * 4 + 4]
    return jnp.concatenate([low, high], axis=1).reshape(128, LANES)


def back_far_kernel(in_ref, pp_ref, far_ref):
    first, _ = masks()
    for ch in range(2):
        l, t = FAR[0]
        far_ref[ch * 256 : ch * 256 + 128] = (pp_ref[l, t, ch].T + back_tile(in_ref, l, t, ch)).astype(BF16)
        far_ref[ch * 256 + 128 : ch * 256 + 256] = jnp.where(first, back_tile(in_ref, 0, 0, ch), back_tile(in_ref, 1, 0, ch).T).astype(BF16)
    far_ref[512:528] = jnp.zeros((16, LANES), BF16)


def back_near_kernel(in_ref, pp_ref, plus_ref, minus_ref):
    for ch in range(2):
        for ref, held in ((plus_ref, PLUS), (minus_ref, MINUS)):
            for u, (l, t) in enumerate(held):
                ref[ch * 2 + u] = (pp_ref[l, t, ch].T + back_tile(in_ref, l, t, ch)).astype(BF16)


def finish_kernel(in_ref, plus_ref, minus_ref, far_ref, pp_ref, edge_ref, out_ref):
    panel = lax.axis_index("panel")
    first, diagonal = masks()
    for ch in range(2):
        for l in range(2):

            def put(offset, value):
                out_ref[ch, l * 128 : (l + 1) * 128, pl.ds(tile_at(panel, l, offset), LANES)] = value.astype(BF16)

            value = back_tile(in_ref, l, 0, ch)
            mirrored = value.T
            put(0, pp_ref[l, 0, ch] + jnp.where(first, mirrored, value))
            edge = edge_ref[ch * 2 + l : ch * 2 + l + 1]
            far = far_ref[ch * 256 + 128 : ch * 256 + 256].astype(F32)
            across = jnp.where(first, far if l == 0 else far.T, jnp.where(diagonal, edge, mirrored))
            put(4, pp_ref[l, 4, ch] + across)
            for t in (1, 2, 3):
                put(OFFSETS[t], pp_ref[l, t, ch] + back_tile(in_ref, l, t, ch).T)
            put(2, minus_ref[ch * 2 + l])
            if l == 0:
                put(-1, plus_ref[ch * 2])
                put(-3, far_ref[ch * 256 : ch * 256 + 128])
            else:
                put(-1, pp_ref[0, 1, ch].T + back_tile(in_ref, 0, 1, ch))
                put(-3, plus_ref[ch * 2 + 1])


def contract_first(a, b):
    return lax.dot_general(a, b, (((0,), (0,)), ((), ())), preferred_element_type=F32)


def pair_kernel(eta_ref, gamma_ref, weight_ref, own_ref, plus_ref, far_ref, minus_ref, scaled, plain):
    panel = lax.axis_index("panel")
    for ch in range(2):
        for l in range(2):
            row = weight_ref[ch : ch + 1, pl.ds(tile_at(panel, l, 0), LANES)]
            weight = jnp.broadcast_to(row, (128, LANES)).T
            rows = slice(l * 128, (l + 1) * 128)
            for j in range(8):
                source = pl.ds(tile_at(panel, j, 0), LANES)
                columns = slice(j * LANES, (j + 1) * LANES)
                scaled[ch, rows, columns] = (eta_ref[ch, rows, source].astype(F32) * weight).astype(BF16)
                plain[ch, rows, columns] = gamma_ref[ch, rows, source]
        for owner, ref in enumerate((own_ref, plus_ref, far_ref, minus_ref)):
            columns = slice(owner * 256, (owner + 1) * 256)
            total = contract_first(scaled[ch, :, columns], plain[ch]) + contract_first(plain[ch, :, columns], scaled[ch])
            for l in range(2):
                for t, offset in enumerate(OFFSETS):
                    column = (2 * owner + l + offset) % 8 * LANES
                    ref[l, t, ch] = -total[l * 128 : (l + 1) * 128, column : column + LANES].astype(BF16)


def pair_sum_kernel(own_ref, plus_ref, far_ref, minus_ref, out_ref):
    for l in range(2):
        for t in range(5):
            for ch in range(2):
                parts = [ref[l, t, ch].astype(F32) for ref in (own_ref, plus_ref, far_ref, minus_ref)]
                out_ref[l, t, ch] = (parts[0] + parts[1]) + (parts[2] + parts[3])


def call(kernel, shapes, args, flops=0, scratch=(), name=None, dtype=BF16, space=None):
    single = not isinstance(shapes, list)
    outs = [shapes] if single else shapes
    types = dtype if isinstance(dtype, list) else [dtype] * len(outs)
    shaped = [jax.ShapeDtypeStruct(s, d) for s, d in zip(outs, types)]
    size = sum(a.size * a.dtype.itemsize for a in [*args, *shaped])
    return pl.pallas_call(
        kernel,
        out_shape=shaped[0] if single else shaped,
        in_specs=[pl.BlockSpec(memory_space=space or pltpu.VMEM)] * len(args),
        out_specs=jax.tree.map(lambda _: pl.BlockSpec(memory_space=space or pltpu.VMEM), shaped[0] if single else shaped),
        scratch_shapes=list(scratch),
        compiler_params=params(60 if space else 24),
        cost_estimate=cost(flops, size),
        name=name,
    )(*args)


def exchange(operand, axis):
    return lax.all_to_all(operand, axis, split_axis=0, concat_axis=0, tiled=True)


def step(value, by):
    return lax.ppermute(value, "panel", [(i, (i + by) % 4) for i in range(4)])


def mirror(plus, minus, far):
    return step(plus, 1), step(minus, 3), step(far, 2)


def route(value, by, places):
    pairs = []
    for chan in range(64):
        for here in places:
            panel = (here + chan % 2) % 4
            pairs.append((chan * 4 + panel, chan * 4 + (panel + by) % 4))
    return lax.ppermute(value, ("chan", "panel"), pairs)


def to_owner(plus, minus, far):
    return route(plus, 1, (1, 3)), route(minus, 3, (1, 3)), route(far, 2, (0, 2))


def from_owner(plus, far, minus):
    return route(plus, 1, (0, 2)), route(far, 2, (0, 2)), route(minus, 3, (0, 2))


def shards(eta, gamma, pp_weight, cc_weight, live_pairs, forward_table, back_table):
    positions = lax.broadcasted_iota(jnp.int32, pp_weight.shape, 1)
    weight_pp = jnp.where(positions < live_pairs[:, None], pp_weight, F32(0.0))
    packed = call(
        pack_kernel,
        (64, 64, LANES),
        (eta, gamma),
        scratch=[
            pltpu.VMEM((2, 2, 256, 1024), BF16),
            pltpu.VMEM((64, 64, LANES), BF16),
            pltpu.SemaphoreType.DMA((2, 2, 2)),
            pltpu.SemaphoreType.DMA((2, 2)),
        ],
        name="pack",
        space=pltpu.HBM,
    )
    forward_wide, back_wide, edge_wide = call(spread_kernel, [(512, 512), (512, 512), (256, 256)], (forward_table, back_table), flops=300_000_000, name="spread")
    packed = exchange(packed, "chan")
    pp_own, *pp = call(
        pair_kernel,
        [(2, 5, 2, 128, LANES)] * 4,
        (eta, gamma, weight_pp),
        flops=2_200_000_000,
        scratch=[pltpu.VMEM((2, 256, 1024), BF16)] * 2,
        name="pair",
    )
    pp_plus, pp_minus = step(pp[0], 1), step(pp[2], 3)
    packed, pp_own, pp_far, pp_plus, pp_minus = lax.optimization_barrier((packed, pp_own, pp[1], pp_plus, pp_minus))
    mixed = call(recouple_kernel, (64, 64, LANES), (forward_wide, packed), flops=700_000_000, name="recouple")
    mixed = exchange(mixed, "chan")
    pp_far = step(pp_far, 2)
    pp_part = call(pair_sum_kernel, (2, 5, 2, 128, LANES), (pp_own, pp_plus, pp_far, pp_minus), name="pair_sum", dtype=F32)
    mixed, pp_part = lax.optimization_barrier((mixed, pp_part))
    far = call(send_far_kernel, (64, 32, LANES), (mixed,), name="send_far")
    mixed, far = lax.optimization_barrier((mixed, far))
    near = call(send_near_kernel, [(64, 32, LANES)] * 2, (mixed,), name="send_near")
    received = to_owner(*near, far)
    own, *outs = call(
        product_kernel,
        [(1040, LANES), (1040, LANES), (1056, LANES), (1040, LANES)],
        (mixed, *received, cc_weight),
        flops=2_200_000_000,
        scratch=[pltpu.VMEM((1024, 1024), BF16)] * 2 + [pltpu.VMEM((1024, 1024), F32)],
        name="product",
    )
    outs = from_owner(*outs)
    part = call(part_kernel, (64, 40, LANES), (own, *outs), name="part")
    part = exchange(part, "chan")
    part, edge = call(
        recouple_back_kernel,
        [(64, 32, LANES), (4, LANES)],
        (back_wide, edge_wide, part),
        flops=400_000_000,
        scratch=[pltpu.VMEM((256, LANES), F32)],
        name="recouple_back",
        dtype=[BF16, F32],
    )
    part = exchange(part, "chan")
    far = call(back_far_kernel, (528, LANES), (part, pp_part), name="back_far")
    part, far = lax.optimization_barrier((part, far))
    near = call(back_near_kernel, [(4, 128, LANES)] * 2, (part, pp_part), name="back_near")
    back_received = mirror(*near, far)
    return call(finish_kernel, (2, 256, 1024), (part, *back_received, pp_part, edge), name="finish")


def solution(mesh):
    in_specs = (
        P("chan", "panel", None),
        P("chan", "panel", None),
        P("chan", None),
        P("chan", None),
        P("chan"),
        P(),
        P(),
    )
    out_specs = P("chan", "panel", None)
    return jax.shard_map(shards, mesh=mesh, in_specs=in_specs, out_specs=out_specs, check_vma=False)
```

```python
import jax
import jax.numpy as jnp
from jax import lax
from jax.experimental import pallas as pl
from jax.experimental.pallas import tpu as pltpu
from jax.sharding import PartitionSpec as P

BF16 = jnp.bfloat16
F32 = jnp.float32
OFFSETS = (0, 1, -2, 3, 4)
LANES = 128


def params(mib=24):
    return pltpu.CompilerParams(vmem_limit_bytes=mib * 1024 * 1024)


def cost(flops, size):
    return pl.CostEstimate(flops=flops, bytes_accessed=size, transcendentals=0)


def tile_at(panel, l, offset):
    return pl.multiple_of(lax.rem(2 * panel + l + offset + 8, 8) * LANES, LANES)


def swap_blocks(x):
    lane = lax.broadcasted_iota(jnp.int32, (64, LANES), 1)
    top, bottom = x[:64], x[64:]
    low = lane < 64
    upper = jnp.where(low, top, pltpu.roll(bottom, 64, 1))
    lower = jnp.where(low, pltpu.roll(top, 64, 1), bottom)
    even = (lane[:32] & 32) == 0
    parts = []
    for half in (upper, lower):
        first, second = half[:32], half[32:]
        parts.append(jnp.where(even, first, pltpu.roll(second, 32, 1)))
        parts.append(jnp.where(even, pltpu.roll(first, 96, 1), second))
    return jnp.concatenate(parts, axis=0)


def masks():
    row = lax.broadcasted_iota(jnp.int32, (128, LANES), 0)
    column = lax.broadcasted_iota(jnp.int32, (128, LANES), 1)
    row_block, column_block = row >> 5, column >> 5
    return (row_block > column_block) | ((row_block == column_block) & (row < column)), row == column


def contract_last(a, b):
    return lax.dot_general(a, b, (((1,), (1,)), ((), ())), preferred_element_type=F32)


def interleave(both):
    return [jnp.concatenate([both[0][:, r : r + 4], both[1][:, r : r + 4]], axis=1) for r in (0, 4)]


SOURCE = ((2, 0, 0, 0, 3, 0, 1, 1), (1, 2, 0, 0, 1, 3, 1, 1))


def pack_kernel(eta_ref, gamma_ref, out_ref, held, ready, sems, out_sems):
    panel = lax.axis_index("panel")
    either = jnp.where(panel < 2, 0, 1)
    row = lax.broadcasted_iota(jnp.int32, (128, LANES), 0)
    column = lax.broadcasted_iota(jnp.int32, (128, LANES), 1)
    copies = {}
    for l in range(2):
        for ch in range(2):
            for arr, ref in enumerate((eta_ref, gamma_ref)):
                rows = slice(l * 128, (l + 1) * 128)
                copy = pltpu.make_async_copy(ref.at[ch, rows], held.at[arr, ch, rows], sems.at[l, ch, arr])
                copy.start()
                copies[l, ch, arr] = copy

    def tile(ch, l, j):
        def read(arr):
            return held[arr, ch, l * 128 : (l + 1) * 128, pl.ds(tile_at(panel, j, 0), LANES)]

        kind = SOURCE[l][j]
        value = jnp.where(row < column, read(0), read(1)) if kind == 2 else read(either if kind == 3 else kind)
        return swap_blocks(value).astype(F32).reshape(16, 8, LANES)

    for l in range(2):
        for ch in range(2):
            for arr in range(2):
                copies[l, ch, arr].wait()
        for part in range(2):
            pieces = []
            for j in range(part * 4, part * 4 + 4):
                pieces += interleave([tile(ch, l, j) for ch in range(2)])
            rows = slice(part * 32 + l * 16, part * 32 + l * 16 + 16)
            ready[rows] = jnp.concatenate(pieces, axis=1).astype(BF16)
            copies[l, part] = pltpu.make_async_copy(ready.at[rows], out_ref.at[rows], out_sems.at[l, part])
            copies[l, part].start()
    for l in range(2):
        for part in range(2):
            copies[l, part].wait()


def spread_kernel(forward_ref, back_ref, forward_out, back_out, edge_out):
    for ref, out, shift in ((forward_ref, forward_out, 2), (back_ref, back_out, 2), (back_ref, edge_out, 1)):
        size = 128 << shift
        row = lax.broadcasted_iota(jnp.int32, (size, 128), 0) >> shift
        column = lax.broadcasted_iota(jnp.int32, (size, 128), 1)
        copies = jnp.where(row == column, F32(1.0), F32(0.0)).astype(BF16)
        tall = jnp.dot(copies, ref[...], preferred_element_type=F32).astype(BF16)
        mask = (1 << shift) - 1
        for start in range(0, size, 256):
            wide = contract_last(tall[start : start + 256], copies)
            row = lax.broadcasted_iota(jnp.int32, wide.shape, 0) & mask
            column = lax.broadcasted_iota(jnp.int32, wide.shape, 1) & mask
            out[start : start + 256, :] = jnp.where(row == column, wide, F32(0.0)).astype(BF16)


def recouple_rows(table_ref, in_ref, count):
    value = in_ref[...].astype(F32)
    rhs = jnp.concatenate([value[:, q * 8 : q * 8 + 8].reshape(512, LANES) for q in range(count)], axis=1).astype(BF16)
    mixed = jnp.dot(table_ref[...], rhs, preferred_element_type=F32)
    return [mixed[:, q * LANES : (q + 1) * LANES].reshape(64, 8, LANES) for q in range(count)]


def recouple_kernel(table_ref, in_ref, out_ref):
    pieces = recouple_rows(table_ref, in_ref, 8)
    for ch in range(2):
        rows = [piece[:, ch * 4 : ch * 4 + 4] for piece in pieces]
        out_ref[:, ch * 32 : ch * 32 + 32] = jnp.concatenate(rows, axis=1).astype(BF16)


PLUS = ((1, 1), (0, 3))
MINUS = ((0, 2), (1, 2))
FAR = ((1, 3),)


def place():
    return lax.rem(lax.axis_index("panel") + 4 - lax.rem(lax.axis_index("chan"), 2), 4)


def channel_rows(ref, ch):
    return ref[:, pl.ds(pl.multiple_of(ch * 32, 32), 32), :]


def send_far_kernel(in_ref, far_ref):
    far_ref[...] = channel_rows(in_ref, jnp.where(place() == 0, 1, 0))


def send_near_kernel(in_ref, plus_ref, minus_ref):
    here = place()
    plus_ref[...] = channel_rows(in_ref, jnp.where(here == 1, 1, 0))
    minus_ref[...] = channel_rows(in_ref, jnp.where(here == 1, 0, 1))


def tile_of(ref, l, j, first=0):
    start = j // 4 * 32 + l * 16
    return ref[start : start + 16, pl.ds(first, 32), :].astype(F32)[:, j % 4 * 8 : j % 4 * 8 + 8].reshape(128, LANES)


def product_kernel(in_ref, plus_ref, minus_ref, far_ref, weight_ref, own_out, plus_out, far_out, minus_out, scaled, plain, forward):
    panel = lax.axis_index("panel")
    own = jnp.where(place() == 2, 1, 0)

    def tile(r, c):
        b, l = divmod(r, 2)
        j = (c - 2 * b) % 8
        if b == 0:
            return tile_of(in_ref, l, j, pl.multiple_of(own * 32, 32))
        return tile_of((minus_ref, far_ref, plus_ref)[b - 1], l, j)

    lanes = []
    for j in range(8):
        columns = pl.ds(tile_at(panel, j, 0), LANES)
        lanes.append(jnp.where(own == 0, weight_ref[0:1, columns], weight_ref[1:2, columns]))

    def put(ref, r, c, value):
        if ref is scaled:
            value = value * lanes[c]
        ref[r * 128 : (r + 1) * 128, c * LANES : (c + 1) * LANES] = value.astype(BF16)

    first, diagonal = masks()
    for r in range(8):
        value = tile(r, r)
        mirrored = value.T
        put(scaled, r, r, jnp.where(diagonal, F32(0.0), jnp.where(first, -value, mirrored)))
        put(plain, r, r, jnp.where(first, mirrored, value))
    for r in range(8):
        for step in (1, 2, 3, 4):
            c = (r + step) % 8
            if step == 4:
                if r >= 4:
                    continue
                one, other = tile(r, c), tile(c, r)
                is_eta = lax.rem(panel + r // 2, 4) < 2
                one_t, other_t = one.T, other.T
                put(scaled, r, c, jnp.where(is_eta, one_t, -other))
                put(scaled, c, r, jnp.where(is_eta, -one, other_t))
                put(plain, r, c, jnp.where(is_eta, other, one_t))
                put(plain, c, r, jnp.where(is_eta, other_t, one))
                continue
            p, q = (r, c) if SOURCE[r % 2][(c - r // 2 * 2) % 8] == 0 else (c, r)
            value = tile(p, q)
            put(scaled, q, p, -value)
            put(scaled, p, q, value.T)
            value = tile(q, p)
            put(plain, p, q, value)
            put(plain, q, p, value.T)
    for b in range(4):
        forward[b * 256 : (b + 1) * 256, :] = contract_last(scaled[b * 256 : (b + 1) * 256], plain[...])

    def product(r, offset):
        c = (r + offset) % 8
        value = forward[r * 128 : (r + 1) * 128, c * LANES : (c + 1) * LANES]
        return value + forward[c * 128 : (c + 1) * 128, r * LANES : (r + 1) * LANES].T

    above = lax.broadcasted_iota(jnp.int32, (128, LANES), 0) < lax.broadcasted_iota(jnp.int32, (128, LANES), 1)
    for b, ref in enumerate((own_out, plus_out, far_out, minus_out)):
        edges = []
        for l in range(2):
            r = 2 * b + l
            across = product(r, 4)
            edges.append(jnp.sum(jnp.where(diagonal, across, F32(0.0)), axis=0, keepdims=True))
            tiles = [jnp.where(above, across, product(r, 0))] + [product(r, offset) for offset in OFFSETS[1:4]]
            for t, value in enumerate(tiles):
                start = (l * 4 + t) * 128
                ref[start : start + 128] = value.astype(BF16)
        if b == 2:
            ref[1040:1056] = jnp.zeros((16, LANES), BF16)
        ref[1024:1040] = jnp.concatenate(edges + [jnp.zeros((14, LANES), F32)], axis=0).astype(BF16)


def part_kernel(own_ref, plus_ref, far_ref, minus_ref, out_ref):
    here = place()
    orders = ((own_ref, plus_ref, far_ref, minus_ref), (far_ref, minus_ref, own_ref, plus_ref))

    def pick(ch, start, size):
        value = orders[ch][0][start : start + size]
        for k in range(1, 4):
            value = jnp.where(here == k, orders[ch][k][start : start + size], value)
        return value

    edges = [pick(ch, 1024, 16).astype(F32)[:2] for ch in range(2)]
    edges = jnp.concatenate(edges + [jnp.zeros((4, LANES), F32)], axis=0)
    edges = jnp.broadcast_to(edges[None], (16, 8, LANES))
    for l in range(2):
        low, high = [], []
        for t in range(4):
            both = [swap_blocks(pick(ch, (l * 4 + t) * 128, 128)).astype(F32).reshape(16, 8, LANES) for ch in range(2)]
            pieces = interleave(both)
            low.append(pieces[0])
            high.append(pieces[1])
        out_ref[l * 32 : l * 32 + 16] = jnp.concatenate(low + [edges], axis=1).astype(BF16)
        out_ref[l * 32 + 16 : l * 32 + 32] = jnp.concatenate(high + [edges], axis=1).astype(BF16)


def recouple_back_kernel(table_ref, edge_table_ref, in_ref, out_ref, edge_ref, mixed):
    out_ref[...] = jnp.concatenate(recouple_rows(table_ref, in_ref, 4), axis=1).astype(BF16)
    edges = in_ref[...].astype(F32)[:, 32:40].reshape(32, 2, 8, LANES)
    edges = jnp.concatenate([edges[:, 0, :4], edges[:, 1, :4]], axis=1).reshape(256, LANES).astype(BF16)
    mixed[...] = jnp.dot(edge_table_ref[...], edges, preferred_element_type=F32).astype(BF16).astype(F32)
    edge_ref[...] = mixed[pl.ds(pl.multiple_of(lax.axis_index("chan") * 4, 4), 4), :]


def back_tile(ref, l, t, ch):
    low = ref[l * 32 : l * 32 + 16].astype(F32)[:, t * 8 + ch * 4 : t * 8 + ch * 4 + 4]
    high = ref[l * 32 + 16 : l * 32 + 32].astype(F32)[:, t * 8 + ch * 4 : t * 8 + ch * 4 + 4]
    return jnp.concatenate([low, high], axis=1).reshape(128, LANES)


def back_far_kernel(in_ref, pp_ref, far_ref):
    first, _ = masks()
    for ch in range(2):
        l, t = FAR[0]
        far_ref[ch * 256 : ch * 256 + 128] = (pp_ref[l, t, ch].T + back_tile(in_ref, l, t, ch)).astype(BF16)
        far_ref[ch * 256 + 128 : ch * 256 + 256] = jnp.where(first, back_tile(in_ref, 0, 0, ch), back_tile(in_ref, 1, 0, ch).T).astype(BF16)
    far_ref[512:528] = jnp.zeros((16, LANES), BF16)


def back_near_kernel(in_ref, pp_ref, plus_ref, minus_ref):
    for ch in range(2):
        for ref, held in ((plus_ref, PLUS), (minus_ref, MINUS)):
            for u, (l, t) in enumerate(held):
                ref[ch * 2 + u] = (pp_ref[l, t, ch].T + back_tile(in_ref, l, t, ch)).astype(BF16)


def finish_kernel(in_ref, plus_ref, minus_ref, far_ref, pp_ref, edge_ref, out_ref):
    panel = lax.axis_index("panel")
    first, diagonal = masks()
    for ch in range(2):
        for l in range(2):

            def put(offset, value):
                out_ref[ch, l * 128 : (l + 1) * 128, pl.ds(tile_at(panel, l, offset), LANES)] = value.astype(BF16)

            value = back_tile(in_ref, l, 0, ch)
            mirrored = value.T
            put(0, pp_ref[l, 0, ch] + jnp.where(first, mirrored, value))
            edge = edge_ref[ch * 2 + l : ch * 2 + l + 1]
            far = far_ref[ch * 256 + 128 : ch * 256 + 256].astype(F32)
            across = jnp.where(first, far if l == 0 else far.T, jnp.where(diagonal, edge, mirrored))
            put(4, pp_ref[l, 4, ch] + across)
            for t in (1, 2, 3):
                put(OFFSETS[t], pp_ref[l, t, ch] + back_tile(in_ref, l, t, ch).T)
            put(2, minus_ref[ch * 2 + l])
            if l == 0:
                put(-1, plus_ref[ch * 2])
                put(-3, far_ref[ch * 256 : ch * 256 + 128])
            else:
                put(-1, pp_ref[0, 1, ch].T + back_tile(in_ref, 0, 1, ch))
                put(-3, plus_ref[ch * 2 + 1])


def contract_first(a, b):
    return lax.dot_general(a, b, (((0,), (0,)), ((), ())), preferred_element_type=F32)


def pair_kernel(eta_ref, gamma_ref, weight_ref, own_ref, plus_ref, far_ref, minus_ref, scaled, plain):
    panel = lax.axis_index("panel")
    for ch in range(2):
        for l in range(2):
            row = weight_ref[ch : ch + 1, pl.ds(tile_at(panel, l, 0), LANES)]
            weight = jnp.broadcast_to(row, (128, LANES)).T
            rows = slice(l * 128, (l + 1) * 128)
            for j in range(8):
                source = pl.ds(tile_at(panel, j, 0), LANES)
                columns = slice(j * LANES, (j + 1) * LANES)
                scaled[ch, rows, columns] = (eta_ref[ch, rows, source].astype(F32) * weight).astype(BF16)
                plain[ch, rows, columns] = gamma_ref[ch, rows, source]
        for owner, ref in enumerate((own_ref, plus_ref, far_ref, minus_ref)):
            columns = slice(owner * 256, (owner + 1) * 256)
            total = contract_first(scaled[ch, :, columns], plain[ch]) + contract_first(plain[ch, :, columns], scaled[ch])
            for l in range(2):
                for t, offset in enumerate(OFFSETS):
                    column = (2 * owner + l + offset) % 8 * LANES
                    ref[l, t, ch] = -total[l * 128 : (l + 1) * 128, column : column + LANES].astype(BF16)


def pair_sum_kernel(own_ref, plus_ref, far_ref, minus_ref, out_ref):
    for l in range(2):
        for t in range(5):
            for ch in range(2):
                parts = [ref[l, t, ch].astype(F32) for ref in (own_ref, plus_ref, far_ref, minus_ref)]
                out_ref[l, t, ch] = (parts[0] + parts[1]) + (parts[2] + parts[3])


def call(kernel, shapes, args, flops=0, scratch=(), name=None, dtype=BF16, space=None):
    single = not isinstance(shapes, list)
    outs = [shapes] if single else shapes
    types = dtype if isinstance(dtype, list) else [dtype] * len(outs)
    shaped = [jax.ShapeDtypeStruct(s, d) for s, d in zip(outs, types)]
    size = sum(a.size * a.dtype.itemsize for a in [*args, *shaped])
    return pl.pallas_call(
        kernel,
        out_shape=shaped[0] if single else shaped,
        in_specs=[pl.BlockSpec(memory_space=space or pltpu.VMEM)] * len(args),
        out_specs=jax.tree.map(lambda _: pl.BlockSpec(memory_space=space or pltpu.VMEM), shaped[0] if single else shaped),
        scratch_shapes=list(scratch),
        compiler_params=params(60 if space else 24),
        cost_estimate=cost(flops, size),
        name=name,
    )(*args)


def exchange(operand, axis):
    return lax.all_to_all(operand, axis, split_axis=0, concat_axis=0, tiled=True)


def step(value, by):
    return lax.ppermute(value, "panel", [(i, (i + by) % 4) for i in range(4)])


def mirror(plus, minus, far):
    return step(plus, 1), step(minus, 3), step(far, 2)


def route(value, by, places):
    pairs = []
    for chan in range(64):
        for here in places:
            panel = (here + chan % 2) % 4
            pairs.append((chan * 4 + panel, chan * 4 + (panel + by) % 4))
    return lax.ppermute(value, ("chan", "panel"), pairs)


def to_owner(plus, minus, far):
    return route(plus, 1, (1, 3)), route(minus, 3, (1, 3)), route(far, 2, (0, 2))


def from_owner(plus, far, minus):
    return route(plus, 1, (0, 2)), route(far, 2, (0, 2)), route(minus, 3, (0, 2))


def shards(eta, gamma, pp_weight, cc_weight, live_pairs, forward_table, back_table):
    positions = lax.broadcasted_iota(jnp.int32, pp_weight.shape, 1)
    weight_pp = jnp.where(positions < live_pairs[:, None], pp_weight, F32(0.0))
    packed = call(
        pack_kernel,
        (64, 64, LANES),
        (eta, gamma),
        scratch=[
            pltpu.VMEM((2, 2, 256, 1024), BF16),
            pltpu.VMEM((64, 64, LANES), BF16),
            pltpu.SemaphoreType.DMA((2, 2, 2)),
            pltpu.SemaphoreType.DMA((2, 2)),
        ],
        name="pack",
        space=pltpu.HBM,
    )
    forward_wide, back_wide, edge_wide = call(spread_kernel, [(512, 512), (512, 512), (256, 256)], (forward_table, back_table), flops=300_000_000, name="spread")
    packed = exchange(packed, "chan")
    pp_own, *pp = call(
        pair_kernel,
        [(2, 5, 2, 128, LANES)] * 4,
        (eta, gamma, weight_pp),
        flops=2_200_000_000,
        scratch=[pltpu.VMEM((2, 256, 1024), BF16)] * 2,
        name="pair",
    )
    pp_plus, pp_minus = step(pp[0], 1), step(pp[2], 3)
    packed, pp_own, pp_far, pp_plus, pp_minus = lax.optimization_barrier((packed, pp_own, pp[1], pp_plus, pp_minus))
    mixed = call(recouple_kernel, (64, 64, LANES), (forward_wide, packed), flops=700_000_000, name="recouple")
    mixed = exchange(mixed, "chan")
    pp_far = step(pp_far, 2)
    pp_part = call(pair_sum_kernel, (2, 5, 2, 128, LANES), (pp_own, pp_plus, pp_far, pp_minus), name="pair_sum", dtype=F32)
    mixed, pp_part = lax.optimization_barrier((mixed, pp_part))
    far = call(send_far_kernel, (64, 32, LANES), (mixed,), name="send_far")
    mixed, far = lax.optimization_barrier((mixed, far))
    near = call(send_near_kernel, [(64, 32, LANES)] * 2, (mixed,), name="send_near")
    received = to_owner(*near, far)
    own, *outs = call(
        product_kernel,
        [(1040, LANES), (1040, LANES), (1056, LANES), (1040, LANES)],
        (mixed, *received, cc_weight),
        flops=2_200_000_000,
        scratch=[pltpu.VMEM((1024, 1024), BF16)] * 2 + [pltpu.VMEM((1024, 1024), F32)],
        name="product",
    )
    outs = from_owner(*outs)
    part = call(part_kernel, (64, 40, LANES), (own, *outs), name="part")
    part = exchange(part, "chan")
    part, edge = call(
        recouple_back_kernel,
        [(64, 32, LANES), (4, LANES)],
        (back_wide, edge_wide, part),
        flops=400_000_000,
        scratch=[pltpu.VMEM((256, LANES), F32)],
        name="recouple_back",
        dtype=[BF16, F32],
    )
    part = exchange(part, "chan")
    far = call(back_far_kernel, (528, LANES), (part, pp_part), name="back_far")
    part, far = lax.optimization_barrier((part, far))
    near = call(back_near_kernel, [(4, 128, LANES)] * 2, (part, pp_part), name="back_near")
    back_received = mirror(*near, far)
    return call(finish_kernel, (2, 256, 1024), (part, *back_received, pp_part, edge), name="finish")


def solution(mesh):
    in_specs = (
        P("chan", "panel", None),
        P("chan", "panel", None),
        P("chan", None),
        P("chan", None),
        P("chan"),
        P(),
        P(),
    )
    out_specs = P("chan", "panel", None)
    return jax.shard_map(shards, mesh=mesh, in_specs=in_specs, out_specs=out_specs, check_vma=False)
```

```python
import jax
import jax.numpy as jnp
from jax import lax
from jax.experimental import pallas as pl
from jax.experimental.pallas import tpu as pltpu
from jax.sharding import PartitionSpec as P

BF16 = jnp.bfloat16
F32 = jnp.float32
OFFSETS = (0, 1, -2, 3, 4)
LANES = 128


def params(mib=16):
    return pltpu.CompilerParams(vmem_limit_bytes=mib * 1024 * 1024)


def cost(flops, size):
    return pl.CostEstimate(flops=flops, bytes_accessed=size, transcendentals=0)


def tile_at(panel, l, offset):
    return pl.multiple_of(lax.rem(2 * panel + l + offset + 8, 8) * LANES, LANES)


def swap_blocks(x):
    lane = lax.broadcasted_iota(jnp.int32, (64, LANES), 1)
    top, bottom = x[:64], x[64:]
    low = lane < 64
    upper = jnp.where(low, top, pltpu.roll(bottom, 64, 1))
    lower = jnp.where(low, pltpu.roll(top, 64, 1), bottom)
    even = (lane[:32] & 32) == 0
    parts = []
    for half in (upper, lower):
        first, second = half[:32], half[32:]
        parts.append(jnp.where(even, first, pltpu.roll(second, 32, 1)))
        parts.append(jnp.where(even, pltpu.roll(first, 96, 1), second))
    return jnp.concatenate(parts, axis=0)


def masks():
    row = lax.broadcasted_iota(jnp.int32, (128, LANES), 0)
    column = lax.broadcasted_iota(jnp.int32, (128, LANES), 1)
    row_block, column_block = row >> 5, column >> 5
    return (row_block > column_block) | ((row_block == column_block) & (row < column)), row == column


def contract_last(a, b):
    return lax.dot_general(a, b, (((1,), (1,)), ((), ())), preferred_element_type=F32)


def interleave(both):
    return [jnp.concatenate([both[0][:, r : r + 4], both[1][:, r : r + 4]], axis=1) for r in (0, 4)]


SOURCE = ((2, 0, 0, 0, 3, 0, 1, 1), (1, 2, 0, 0, 1, 3, 1, 1))


def pack_kernel(eta_ref, gamma_ref, out_ref, held, ready, sems, out_sems):
    panel = lax.axis_index("panel")
    either = jnp.where(panel < 2, 0, 1)
    row = lax.broadcasted_iota(jnp.int32, (128, LANES), 0)
    column = lax.broadcasted_iota(jnp.int32, (128, LANES), 1)
    copies = {}
    for l in range(2):
        for ch in range(2):
            for arr, ref in enumerate((eta_ref, gamma_ref)):
                rows = slice(l * 128, (l + 1) * 128)
                copy = pltpu.make_async_copy(ref.at[ch, rows], held.at[arr, ch, rows], sems.at[l, ch, arr])
                copy.start()
                copies[l, ch, arr] = copy

    def tile(ch, l, j):
        def read(arr):
            return held[arr, ch, l * 128 : (l + 1) * 128, pl.ds(tile_at(panel, j, 0), LANES)]

        kind = SOURCE[l][j]
        value = jnp.where(row < column, read(0), read(1)) if kind == 2 else read(either if kind == 3 else kind)
        return swap_blocks(value).astype(F32).reshape(16, 8, LANES)

    for l in range(2):
        for ch in range(2):
            for arr in range(2):
                copies[l, ch, arr].wait()
        for part in range(2):
            pieces = []
            for j in range(part * 4, part * 4 + 4):
                pieces += interleave([tile(ch, l, j) for ch in range(2)])
            rows = slice(part * 32 + l * 16, part * 32 + l * 16 + 16)
            ready[rows] = jnp.concatenate(pieces, axis=1).astype(BF16)
            copies[l, part] = pltpu.make_async_copy(ready.at[rows], out_ref.at[rows], out_sems.at[l, part])
            copies[l, part].start()
    for l in range(2):
        for part in range(2):
            copies[l, part].wait()


def spread_kernel(forward_ref, back_ref, forward_out, back_out, edge_out):
    for ref, out, shift in ((forward_ref, forward_out, 2), (back_ref, back_out, 2), (back_ref, edge_out, 1)):
        size = 128 << shift
        row = lax.broadcasted_iota(jnp.int32, (size, 128), 0) >> shift
        column = lax.broadcasted_iota(jnp.int32, (size, 128), 1)
        copies = jnp.where(row == column, F32(1.0), F32(0.0)).astype(BF16)
        tall = jnp.dot(copies, ref[...], preferred_element_type=F32).astype(BF16)
        mask = (1 << shift) - 1
        for start in range(0, size, 256):
            wide = contract_last(tall[start : start + 256], copies)
            row = lax.broadcasted_iota(jnp.int32, wide.shape, 0) & mask
            column = lax.broadcasted_iota(jnp.int32, wide.shape, 1) & mask
            out[start : start + 256, :] = jnp.where(row == column, wide, F32(0.0)).astype(BF16)


def recouple_rows(table_ref, in_ref, count):
    value = in_ref[...].astype(F32)
    rhs = jnp.concatenate([value[:, q * 8 : q * 8 + 8].reshape(512, LANES) for q in range(count)], axis=1).astype(BF16)
    mixed = jnp.dot(table_ref[...], rhs, preferred_element_type=F32)
    return [mixed[:, q * LANES : (q + 1) * LANES].reshape(64, 8, LANES) for q in range(count)]


def recouple_kernel(table_ref, in_ref, out_ref):
    pieces = recouple_rows(table_ref, in_ref, 8)
    for ch in range(2):
        rows = [piece[:, ch * 4 : ch * 4 + 4] for piece in pieces]
        out_ref[:, ch * 32 : ch * 32 + 32] = jnp.concatenate(rows, axis=1).astype(BF16)


PLUS = ((1, 1), (0, 3))
MINUS = ((0, 2), (1, 2))
FAR = ((1, 3),)


def place():
    return lax.rem(lax.axis_index("panel") + 4 - lax.rem(lax.axis_index("chan"), 2), 4)


def channel_rows(ref, ch):
    return ref[:, pl.ds(pl.multiple_of(ch * 32, 32), 32), :]


def send_far_kernel(in_ref, far_ref):
    far_ref[...] = channel_rows(in_ref, jnp.where(place() == 0, 1, 0))


def send_near_kernel(in_ref, plus_ref, minus_ref):
    here = place()
    plus_ref[...] = channel_rows(in_ref, jnp.where(here == 1, 1, 0))
    minus_ref[...] = channel_rows(in_ref, jnp.where(here == 1, 0, 1))


def tile_of(ref, l, j, first=0):
    start = j // 4 * 32 + l * 16
    return ref[start : start + 16, pl.ds(first, 32), :].astype(F32)[:, j % 4 * 8 : j % 4 * 8 + 8].reshape(128, LANES)


def product_kernel(in_ref, plus_ref, minus_ref, far_ref, weight_ref, own_out, plus_out, far_out, minus_out, scaled, plain, forward):
    panel = lax.axis_index("panel")
    own = jnp.where(place() == 2, 1, 0)

    def tile(r, c):
        b, l = divmod(r, 2)
        j = (c - 2 * b) % 8
        if b == 0:
            return tile_of(in_ref, l, j, pl.multiple_of(own * 32, 32))
        return tile_of((minus_ref, far_ref, plus_ref)[b - 1], l, j)

    lanes = []
    for j in range(8):
        columns = pl.ds(tile_at(panel, j, 0), LANES)
        lanes.append(jnp.where(own == 0, weight_ref[0:1, columns], weight_ref[1:2, columns]))

    def put(ref, r, c, value):
        if ref is scaled:
            value = value * lanes[c]
        ref[r * 128 : (r + 1) * 128, c * LANES : (c + 1) * LANES] = value.astype(BF16)

    first, diagonal = masks()
    for r in range(8):
        value = tile(r, r)
        mirrored = value.T
        put(scaled, r, r, jnp.where(diagonal, F32(0.0), jnp.where(first, -value, mirrored)))
        put(plain, r, r, jnp.where(first, mirrored, value))
    for r in range(8):
        for step in (1, 2, 3, 4):
            c = (r + step) % 8
            if step == 4:
                if r >= 4:
                    continue
                one, other = tile(r, c), tile(c, r)
                is_eta = lax.rem(panel + r // 2, 4) < 2
                one_t, other_t = one.T, other.T
                put(scaled, r, c, jnp.where(is_eta, one_t, -other))
                put(scaled, c, r, jnp.where(is_eta, -one, other_t))
                put(plain, r, c, jnp.where(is_eta, other, one_t))
                put(plain, c, r, jnp.where(is_eta, other_t, one))
                continue
            p, q = (r, c) if SOURCE[r % 2][(c - r // 2 * 2) % 8] == 0 else (c, r)
            value = tile(p, q)
            put(scaled, q, p, -value)
            put(scaled, p, q, value.T)
            value = tile(q, p)
            put(plain, p, q, value)
            put(plain, q, p, value.T)
    for b in range(4):
        forward[b * 256 : (b + 1) * 256, :] = contract_last(scaled[b * 256 : (b + 1) * 256], plain[...])

    def product(r, offset):
        c = (r + offset) % 8
        value = forward[r * 128 : (r + 1) * 128, c * LANES : (c + 1) * LANES]
        return value + forward[c * 128 : (c + 1) * 128, r * LANES : (r + 1) * LANES].T

    above = lax.broadcasted_iota(jnp.int32, (128, LANES), 0) < lax.broadcasted_iota(jnp.int32, (128, LANES), 1)
    for b, ref in enumerate((own_out, plus_out, far_out, minus_out)):
        edges = []
        for l in range(2):
            r = 2 * b + l
            across = product(r, 4)
            edges.append(jnp.sum(jnp.where(diagonal, across, F32(0.0)), axis=0, keepdims=True))
            tiles = [jnp.where(above, across, product(r, 0))] + [product(r, offset) for offset in OFFSETS[1:4]]
            for t, value in enumerate(tiles):
                start = (l * 4 + t) * 128
                ref[start : start + 128] = value.astype(BF16)
        if b == 2:
            ref[1040:1056] = jnp.zeros((16, LANES), BF16)
        ref[1024:1040] = jnp.concatenate(edges + [jnp.zeros((14, LANES), F32)], axis=0).astype(BF16)


def part_kernel(own_ref, plus_ref, far_ref, minus_ref, out_ref):
    here = place()
    orders = ((own_ref, plus_ref, far_ref, minus_ref), (far_ref, minus_ref, own_ref, plus_ref))

    def pick(ch, start, size):
        value = orders[ch][0][start : start + size]
        for k in range(1, 4):
            value = jnp.where(here == k, orders[ch][k][start : start + size], value)
        return value

    edges = [pick(ch, 1024, 16).astype(F32)[:2] for ch in range(2)]
    edges = jnp.concatenate(edges + [jnp.zeros((4, LANES), F32)], axis=0)
    edges = jnp.broadcast_to(edges[None], (16, 8, LANES))
    for l in range(2):
        low, high = [], []
        for t in range(4):
            both = [swap_blocks(pick(ch, (l * 4 + t) * 128, 128)).astype(F32).reshape(16, 8, LANES) for ch in range(2)]
            pieces = interleave(both)
            low.append(pieces[0])
            high.append(pieces[1])
        out_ref[l * 32 : l * 32 + 16] = jnp.concatenate(low + [edges], axis=1).astype(BF16)
        out_ref[l * 32 + 16 : l * 32 + 32] = jnp.concatenate(high + [edges], axis=1).astype(BF16)


def recouple_back_kernel(table_ref, edge_table_ref, in_ref, out_ref, edge_ref, mixed):
    out_ref[...] = jnp.concatenate(recouple_rows(table_ref, in_ref, 4), axis=1).astype(BF16)
    edges = in_ref[...].astype(F32)[:, 32:40].reshape(32, 2, 8, LANES)
    edges = jnp.concatenate([edges[:, 0, :4], edges[:, 1, :4]], axis=1).reshape(256, LANES).astype(BF16)
    mixed[...] = jnp.dot(edge_table_ref[...], edges, preferred_element_type=F32).astype(BF16).astype(F32)
    edge_ref[...] = mixed[pl.ds(pl.multiple_of(lax.axis_index("chan") * 4, 4), 4), :]


def back_tile(ref, l, t, ch):
    low = ref[l * 32 : l * 32 + 16].astype(F32)[:, t * 8 + ch * 4 : t * 8 + ch * 4 + 4]
    high = ref[l * 32 + 16 : l * 32 + 32].astype(F32)[:, t * 8 + ch * 4 : t * 8 + ch * 4 + 4]
    return jnp.concatenate([low, high], axis=1).reshape(128, LANES)


def back_far_kernel(in_ref, pp_ref, far_ref):
    first, _ = masks()
    for ch in range(2):
        l, t = FAR[0]
        far_ref[ch * 256 : ch * 256 + 128] = (pp_ref[l, t, ch].T + back_tile(in_ref, l, t, ch)).astype(BF16)
        far_ref[ch * 256 + 128 : ch * 256 + 256] = jnp.where(first, back_tile(in_ref, 0, 0, ch), back_tile(in_ref, 1, 0, ch).T).astype(BF16)
    far_ref[512:528] = jnp.zeros((16, LANES), BF16)


def back_near_kernel(in_ref, pp_ref, plus_ref, minus_ref):
    for ch in range(2):
        for ref, held in ((plus_ref, PLUS), (minus_ref, MINUS)):
            for u, (l, t) in enumerate(held):
                ref[ch * 2 + u] = (pp_ref[l, t, ch].T + back_tile(in_ref, l, t, ch)).astype(BF16)


def finish_kernel(in_ref, plus_ref, minus_ref, far_ref, pp_ref, edge_ref, out_ref):
    panel = lax.axis_index("panel")
    first, diagonal = masks()
    for ch in range(2):
        for l in range(2):

            def put(offset, value):
                out_ref[ch, l * 128 : (l + 1) * 128, pl.ds(tile_at(panel, l, offset), LANES)] = value.astype(BF16)

            value = back_tile(in_ref, l, 0, ch)
            mirrored = value.T
            put(0, pp_ref[l, 0, ch] + jnp.where(first, mirrored, value))
            edge = edge_ref[ch * 2 + l : ch * 2 + l + 1]
            far = far_ref[ch * 256 + 128 : ch * 256 + 256].astype(F32)
            across = jnp.where(first, far if l == 0 else far.T, jnp.where(diagonal, edge, mirrored))
            put(4, pp_ref[l, 4, ch] + across)
            for t in (1, 2, 3):
                put(OFFSETS[t], pp_ref[l, t, ch] + back_tile(in_ref, l, t, ch).T)
            put(2, minus_ref[ch * 2 + l])
            if l == 0:
                put(-1, plus_ref[ch * 2])
                put(-3, far_ref[ch * 256 : ch * 256 + 128])
            else:
                put(-1, pp_ref[0, 1, ch].T + back_tile(in_ref, 0, 1, ch))
                put(-3, plus_ref[ch * 2 + 1])


def contract_first(a, b):
    return lax.dot_general(a, b, (((0,), (0,)), ((), ())), preferred_element_type=F32)


def pair_kernel(eta_ref, gamma_ref, weight_ref, own_ref, plus_ref, far_ref, minus_ref, scaled, plain):
    panel = lax.axis_index("panel")
    for ch in range(2):
        for l in range(2):
            row = weight_ref[ch : ch + 1, pl.ds(tile_at(panel, l, 0), LANES)]
            weight = jnp.broadcast_to(row, (128, LANES)).T
            rows = slice(l * 128, (l + 1) * 128)
            for j in range(8):
                source = pl.ds(tile_at(panel, j, 0), LANES)
                columns = slice(j * LANES, (j + 1) * LANES)
                scaled[ch, rows, columns] = (eta_ref[ch, rows, source].astype(F32) * weight).astype(BF16)
                plain[ch, rows, columns] = gamma_ref[ch, rows, source]
        for owner, ref in enumerate((own_ref, plus_ref, far_ref, minus_ref)):
            columns = slice(owner * 256, (owner + 1) * 256)
            total = contract_first(scaled[ch, :, columns], plain[ch]) + contract_first(plain[ch, :, columns], scaled[ch])
            for l in range(2):
                for t, offset in enumerate(OFFSETS):
                    column = (2 * owner + l + offset) % 8 * LANES
                    ref[l, t, ch] = -total[l * 128 : (l + 1) * 128, column : column + LANES].astype(BF16)


def pair_sum_kernel(own_ref, plus_ref, far_ref, minus_ref, out_ref):
    for l in range(2):
        for t in range(5):
            for ch in range(2):
                parts = [ref[l, t, ch].astype(F32) for ref in (own_ref, plus_ref, far_ref, minus_ref)]
                out_ref[l, t, ch] = (parts[0] + parts[1]) + (parts[2] + parts[3])


def call(kernel, shapes, args, flops=0, scratch=(), name=None, dtype=BF16, space=None):
    single = not isinstance(shapes, list)
    outs = [shapes] if single else shapes
    types = dtype if isinstance(dtype, list) else [dtype] * len(outs)
    shaped = [jax.ShapeDtypeStruct(s, d) for s, d in zip(outs, types)]
    size = sum(a.size * a.dtype.itemsize for a in [*args, *shaped])
    return pl.pallas_call(
        kernel,
        out_shape=shaped[0] if single else shaped,
        in_specs=[pl.BlockSpec(memory_space=space or pltpu.VMEM)] * len(args),
        out_specs=jax.tree.map(lambda _: pl.BlockSpec(memory_space=space or pltpu.VMEM), shaped[0] if single else shaped),
        scratch_shapes=list(scratch),
        compiler_params=params(60 if space else 16),
        cost_estimate=cost(flops, size),
        name=name,
    )(*args)


def exchange(operand, axis):
    return lax.all_to_all(operand, axis, split_axis=0, concat_axis=0, tiled=True)


def step(value, by):
    return lax.ppermute(value, "panel", [(i, (i + by) % 4) for i in range(4)])


def mirror(plus, minus, far):
    return step(plus, 1), step(minus, 3), step(far, 2)


def route(value, by, places):
    pairs = []
    for chan in range(64):
        for here in places:
            panel = (here + chan % 2) % 4
            pairs.append((chan * 4 + panel, chan * 4 + (panel + by) % 4))
    return lax.ppermute(value, ("chan", "panel"), pairs)


def to_owner(plus, minus, far):
    return route(plus, 1, (1, 3)), route(minus, 3, (1, 3)), route(far, 2, (0, 2))


def from_owner(plus, far, minus):
    return route(plus, 1, (0, 2)), route(far, 2, (0, 2)), route(minus, 3, (0, 2))


def shards(eta, gamma, pp_weight, cc_weight, live_pairs, forward_table, back_table):
    positions = lax.broadcasted_iota(jnp.int32, pp_weight.shape, 1)
    weight_pp = jnp.where(positions < live_pairs[:, None], pp_weight, F32(0.0))
    packed = call(
        pack_kernel,
        (64, 64, LANES),
        (eta, gamma),
        scratch=[
            pltpu.VMEM((2, 2, 256, 1024), BF16),
            pltpu.VMEM((64, 64, LANES), BF16),
            pltpu.SemaphoreType.DMA((2, 2, 2)),
            pltpu.SemaphoreType.DMA((2, 2)),
        ],
        name="pack",
        space=pltpu.HBM,
    )
    forward_wide, back_wide, edge_wide = call(spread_kernel, [(512, 512), (512, 512), (256, 256)], (forward_table, back_table), flops=300_000_000, name="spread")
    packed = exchange(packed, "chan")
    pp_own, *pp = call(
        pair_kernel,
        [(2, 5, 2, 128, LANES)] * 4,
        (eta, gamma, weight_pp),
        flops=2_200_000_000,
        scratch=[pltpu.VMEM((2, 256, 1024), BF16)] * 2,
        name="pair",
    )
    pp_plus, pp_minus = step(pp[0], 1), step(pp[2], 3)
    packed, pp_own, pp_far, pp_plus, pp_minus = lax.optimization_barrier((packed, pp_own, pp[1], pp_plus, pp_minus))
    mixed = call(recouple_kernel, (64, 64, LANES), (forward_wide, packed), flops=700_000_000, name="recouple")
    mixed = exchange(mixed, "chan")
    pp_far = step(pp_far, 2)
    pp_part = call(pair_sum_kernel, (2, 5, 2, 128, LANES), (pp_own, pp_plus, pp_far, pp_minus), name="pair_sum", dtype=F32)
    mixed, pp_part = lax.optimization_barrier((mixed, pp_part))
    far = call(send_far_kernel, (64, 32, LANES), (mixed,), name="send_far")
    mixed, far = lax.optimization_barrier((mixed, far))
    near = call(send_near_kernel, [(64, 32, LANES)] * 2, (mixed,), name="send_near")
    received = to_owner(*near, far)
    own, *outs = call(
        product_kernel,
        [(1040, LANES), (1040, LANES), (1056, LANES), (1040, LANES)],
        (mixed, *received, cc_weight),
        flops=2_200_000_000,
        scratch=[pltpu.VMEM((1024, 1024), BF16)] * 2 + [pltpu.VMEM((1024, 1024), F32)],
        name="product",
    )
    outs = from_owner(*outs)
    part = call(part_kernel, (64, 40, LANES), (own, *outs), name="part")
    part = exchange(part, "chan")
    part, edge = call(
        recouple_back_kernel,
        [(64, 32, LANES), (4, LANES)],
        (back_wide, edge_wide, part),
        flops=400_000_000,
        scratch=[pltpu.VMEM((256, LANES), F32)],
        name="recouple_back",
        dtype=[BF16, F32],
    )
    part = exchange(part, "chan")
    far = call(back_far_kernel, (528, LANES), (part, pp_part), name="back_far")
    part, far = lax.optimization_barrier((part, far))
    near = call(back_near_kernel, [(4, 128, LANES)] * 2, (part, pp_part), name="back_near")
    back_received = mirror(*near, far)
    return call(finish_kernel, (2, 256, 1024), (part, *back_received, pp_part, edge), name="finish")


def solution(mesh):
    in_specs = (
        P("chan", "panel", None),
        P("chan", "panel", None),
        P("chan", None),
        P("chan", None),
        P("chan"),
        P(),
        P(),
    )
    out_specs = P("chan", "panel", None)
    return jax.shard_map(shards, mesh=mesh, in_specs=in_specs, out_specs=out_specs, check_vma=False)
```
